128 devices in a mesh: lat: 8 (over y_lo, x), lon: 16 (over z, y_hi, core).
Axes of the slice: x: 4, y: 4 (y_hi: 2, y_lo: 2; y = y_hi * 2 + y_lo), z: 4, core: 2. Of those that a mesh axis runs over, the one named last changes fastest.
Arguments:
- fine: bfloat16 [4, 96, 384, 512], P(None, 'lat', 'lon'), may hold values from -6 to 6
- fine_qkv: bfloat16 [512, 1536], replicated
- fine_out: bfloat16 [512, 512], replicated, may hold values from -0.25 to 0.25
- fine_up: bfloat16 [512, 2048], replicated, may hold values from -0.25 to 0.25
- fine_down: bfloat16 [2048, 512], replicated, may hold values from -0.125 to 0.125
- merge_weight: bfloat16 [2048, 1024], replicated, may hold values from -0.125 to 0.125
- coarse_qkv: bfloat16 [1024, 3072], replicated
- coarse_out: bfloat16 [1024, 1024], replicated, may hold values from -0.1875 to 0.1875
Outputs:
- coarse: bfloat16 [4, 48, 192, 1024], P(None, 'lat', 'lon')
The draws below stay inside these ranges and needn't reach their ends.
All inputs are finite; a program needn't handle non-finite values.
Results may differ from the reference program's by a relative error of at most 0.02.
Values may be sent and summed in bfloat16 or wider, within the bound.
No kernel may reach another device: no remote copies, remote signals or barrier semaphores. Data moves between devices by JAX's collectives and lax.ppermute only.
A program may use at most 192 MiB of HBM per device.

```python
import jax
import jax.numpy as jnp
from jax import lax

C = 512
HEADS = 16
FF = 2048
C2 = 1024
HEADS2 = 32
NLAT = 96
NLON = 384


def lined_weight(key, width, heads, boost):
    first, second = jax.random.split(key)
    base = jnp.clip(jax.random.normal(first, (width, 3 * width), jnp.float32), -6.0, 6.0) * width ** (-0.5)
    size = width // heads
    head_of = jnp.arange(width) // size
    strength = jax.random.uniform(second, (heads,), jnp.float32, 0.5, 2.0) * boost
    chosen = (head_of % 4 == 0) & (boost > 0)
    query = base[:, :width]
    keys = jnp.where(chosen[None, :], query * strength[head_of][None, :], base[:, width:2 * width])
    return jnp.concatenate([query, keys, base[:, 2 * width:]], 1).astype(jnp.bfloat16)


def draw_fine_qkv(key, part):
    key = jax.random.fold_in(key, 1)
    boost = 0.0
    return lined_weight(key, C, HEADS, boost)


def draw_coarse_qkv(key, part):
    key = jax.random.fold_in(key, 2)
    boost = 0.0
    return lined_weight(key, C2, HEADS2, boost)


def block_scale(rng, extent, cuts, low, largest):
    loudness, own = 1.0, jax.random.fold_in(rng, 6)
    for axis_at, parts in cuts:
        heights = jnp.exp(jax.random.uniform(jax.random.fold_in(own, axis_at), (parts,), jnp.float32, low / len(cuts), largest / len(cuts)))
        loudness = loudness * jnp.repeat(heights, extent[axis_at] // parts).reshape([-1 if axis == axis_at else 1 for axis in range(len(extent))])
    return loudness


def noise(key, dims, scale, limit, cuts=(), kind=jnp.bfloat16):
    drawn = jax.random.normal(key, dims, jnp.float32) * scale
    if len(cuts) > 0:
        drawn = block_scale(key, dims, cuts, -0.22, 0.18) * drawn
    return jnp.clip(drawn, min=-limit, max=limit).astype(kind)


def setup_inputs(seed: int = 0) -> dict:
    key_of = jax.random.split(jax.random.key(seed), 9)
    fine = noise(key_of[0], (4, NLAT, NLON, C), 1.0, 6.0, ((1, 8), (2, 16)))
    fine_qkv = draw_fine_qkv(jax.random.fold_in(key_of[8], 71), 0)
    fine_out = noise(key_of[2], (C, C), C ** -0.5, 0.25)
    fine_up = noise(key_of[3], (C, FF), C ** -0.5, 0.25)
    fine_down = noise(key_of[4], (FF, C), FF ** -0.5, 0.125)
    merge_weight = noise(key_of[5], (4 * C, C2), (4 * C) ** -0.5, 0.125)
    coarse_qkv = draw_coarse_qkv(jax.random.fold_in(key_of[8], 71), 0)
    coarse_out = noise(key_of[7], (C2, C2), C2 ** -0.5, 0.1875)
    return {"fine": fine, "fine_qkv": fine_qkv, "fine_out": fine_out, "fine_up": fine_up, "fine_down": fine_down, "merge_weight": merge_weight, "coarse_qkv": coarse_qkv, "coarse_out": coarse_out}


def normalize(values):
    values = values.astype(jnp.float32)
    center = values - lax.optimization_barrier(jnp.mean(values, -1, keepdims=True))
    spread = lax.optimization_barrier(jnp.mean(center * center, -1, keepdims=True))
    return center * lax.rsqrt(spread + 1e-05)

def attend_rows(qkv, lat_valid, heads):
    levels, rows, cols, width = qkv.shape
    chan = width // 3
    size = chan // heads
    row_win = rows // 6
    col_win = cols // 12
    blocks = qkv.reshape(2, 2, row_win, 6, col_win, 12, width).transpose(2, 0, 4, 1, 3, 5, 6)
    blocks = blocks.reshape(row_win, 2 * col_win, 144, width)
    valid_rows = lat_valid.reshape(row_win, 6)
    token = jnp.arange(144)
    level_in = token // 72
    lat_in = token // 12 % 6
    window_level = jnp.arange(2 * col_win) // col_win
    group = jnp.where(window_level[:, None] == 0, 0, 1 + level_in[None, :])
    same = group[:, :, None] == group[:, None, :]

    def one_row(item):
        block, valid = item
        keep = same & valid[lat_in][None, None, :]
        query = block[..., :chan].reshape(-1, 144, heads, size).astype(jnp.float32)
        keys = block[..., chan:2 * chan].reshape(-1, 144, heads, size).astype(jnp.float32)
        values = block[..., 2 * chan:].reshape(-1, 144, heads, size).astype(jnp.float32)
        scores = jnp.einsum('wqhd,wkhd->whqk', query, keys) * size ** (-0.5)
        scores = jnp.where(keep[:, None], scores, -1e+30)
        expo = jnp.exp(scores - lax.optimization_barrier(jnp.max(scores, -1, keepdims=True)))
        weights = (expo / lax.optimization_barrier(jnp.sum(expo, -1, keepdims=True))).astype(jnp.bfloat16)
        attended = jnp.einsum('whqk,wkhd->wqhd', weights.astype(jnp.float32), values)
        return attended.astype(jnp.bfloat16).reshape(-1, 144, chan)
    outputs = lax.map(one_row, (blocks, valid_rows))
    outputs = outputs.reshape(row_win, 2, col_win, 2, 6, 12, chan).transpose(1, 3, 0, 4, 2, 5, 6)
    return outputs.reshape(levels, rows, cols, chan)

def shifted_section(tokens, w_qkv, w_out, heads):
    lat_total = tokens.shape[1]
    normed = normalize(tokens).astype(jnp.bfloat16)
    qkv = jnp.dot(normed, w_qkv, preferred_element_type=jnp.float32).astype(jnp.bfloat16)
    qkv = jnp.roll(jnp.roll(qkv, -1, 0), -6, 2)
    qkv = jnp.pad(qkv, ((0, 0), (3, 3), (0, 0), (0, 0)))
    place = jnp.arange(lat_total + 6) - 3
    valid = (place >= 0) & (place < lat_total)
    mixed = attend_rows(qkv, valid, heads)[:, 3:lat_total + 3]
    mixed = jnp.roll(jnp.roll(mixed, 6, 2), 1, 0)
    return tokens.astype(jnp.float32) + jnp.dot(mixed, w_out, preferred_element_type=jnp.float32)

def reference(fine, fine_qkv, fine_out, fine_up, fine_down, merge_weight, coarse_qkv, coarse_out):
    hidden = shifted_section(fine, fine_qkv, fine_out, HEADS).astype(jnp.bfloat16)

    def feed(level):
        normed = normalize(level).astype(jnp.bfloat16)
        inner = jax.nn.gelu(jnp.dot(normed, fine_up, preferred_element_type=jnp.float32), approximate=False).astype(jnp.bfloat16)
        return (level.astype(jnp.float32) + jnp.dot(inner, fine_down, preferred_element_type=jnp.float32)).astype(jnp.bfloat16)
    block = lax.map(feed, hidden)
    levels, rows, cols, width = block.shape
    pairs = block.reshape(levels, rows // 2, 2, cols // 2, 2, width).transpose(0, 1, 3, 2, 4, 5)
    pairs = pairs.reshape(levels, rows // 2, cols // 2, 4 * width)
    merged = jnp.dot(normalize(pairs).astype(jnp.bfloat16), merge_weight, preferred_element_type=jnp.float32).astype(jnp.bfloat16)
    return shifted_section(merged, coarse_qkv, coarse_out, HEADS2).astype(jnp.bfloat16)
```

```python
import functools
import math

import jax
import jax.numpy as jnp
import numpy as np
from jax import lax
from jax.experimental import pallas as pl
from jax.experimental.pallas import tpu as pltpu
from jax.sharding import PartitionSpec as P

F32 = jnp.float32
BF16 = jnp.bfloat16
HEAD = 32
GROUP = 256
ORDER = (1, 2, 3, 0)
QUADS = ((0, 0), (0, 1), (1, 0), (1, 1))
EXP_SCALE = HEAD ** -0.5 * math.log2(math.e)
MIB = 1024 * 1024


def piece_of(i, j):
    if i >= 3 and j < 6:
        return "lon", (i - 3) * 6 + j
    if i < 3 and j >= 6:
        return "lat", i * 18 + j - 6
    if i < 3 and j < 6:
        return "both", i * 6 + j
    return None, 0


def source_of(i, j):
    i, j = i + 3, j + 6
    if i < 12 and j < 24:
        return "own", (i, j)
    return piece_of(i - 12 if i >= 12 else i, j - 24 if j >= 24 else j)


PIECE_ROWS = {"lon": 56, "lat": 56, "both": 24}


def first_send_tables():
    tables = {name: np.zeros((rows, 288), np.float32) for name, rows in PIECE_ROWS.items()}
    for i in range(12):
        for j in range(24):
            name, at = piece_of(i, j)
            if name is not None:
                tables[name][at, i * 24 + j] = 1
    return tables


def window_tables(quad):
    tables = {"own": np.zeros((72, 288), np.float32)}
    for name, rows in PIECE_ROWS.items():
        tables[name] = np.zeros((72, rows), np.float32)
    for r in range(6):
        for c in range(12):
            name, at = source_of(quad[0] * 6 + r, quad[1] * 12 + c)
            if name == "own":
                at = at[0] * 24 + at[1]
            tables[name][r * 12 + c, at] = 1
    return {name: table for name, table in tables.items() if table.any()}


def second_send_tables(quad):
    tables = {name: np.zeros((rows, 72), np.float32) for name, rows in PIECE_ROWS.items()}
    for r in range(6):
        for c in range(12):
            name, at = piece_of(quad[0] * 6 + r, quad[1] * 12 + c)
            if name is not None:
                tables[name][at, r * 12 + c] = 1
    return {name: table for name, table in tables.items() if table.any()}


def pair_tables():
    tables = {quad: np.zeros((288, 72), np.float32) for quad in QUADS}
    for name, rows in PIECE_ROWS.items():
        tables[name] = np.zeros((288, rows), np.float32)
    for i in range(12):
        for j in range(24):
            to = ((i % 2) * 2 + j % 2) * 72 + (i // 2) * 12 + j // 2
            name, at = source_of(i, j)
            if name == "own":
                name, at = (at[0] // 6, at[1] // 12), (at[0] % 6) * 12 + at[1] % 12
            tables[name][to, at] = 1
    return tables


def last_send_table():
    table = np.zeros((288, 288), np.float32)
    for place, level in enumerate(ORDER):
        for i in range(6):
            for j in range(12):
                part = (i // 3) * 2 + j // 6
                table[part * 72 + level * 18 + (i % 3) * 6 + j % 6, place * 72 + i * 12 + j] = 1
    return table


def last_tables():
    tables = np.zeros((4, 384, 72), np.float32)
    for part in range(4):
        for level in range(4):
            for i in range(3):
                for j in range(6):
                    row = i + 3 if part // 2 == 0 else i
                    col = j + 6 if part % 2 == 0 else j
                    tables[part, (level * 6 + row) * 16 + col, level * 18 + i * 6 + j] = 1
    return tables


def side_rows():
    side = np.where(np.arange(72) < 36, 1.0, -1.0)
    pair = np.concatenate([side, side])
    low = np.concatenate([side, np.ones(8)])
    high = np.concatenate([np.ones(8), side])
    return [np.tile(row, 8)[None, :].astype(np.float32) for row in (pair, low, high)]


def dot(a, b):
    return jnp.dot(a, b, preferred_element_type=F32)


def normalize(values):
    center = values - jnp.mean(values, -1, keepdims=True)
    spread = jnp.mean(center * center, -1, keepdims=True)
    return center * lax.rsqrt(spread + 1e-05)


def gelu(x):
    size = jnp.abs(x)
    t = 1.0 / (1.0 + (0.3275911 * 0.5 ** 0.5) * size)
    poly = 0.5 * 1.061405429 * t + (0.5 * -1.453152027)
    poly = poly * t + (0.5 * 1.421413741)
    poly = poly * t + (0.5 * -0.284496736)
    poly = poly * t + (0.5 * 0.254829592)
    tail = jnp.exp2(x * x * (-0.5 * math.log2(math.e))) * (poly * t)
    return jnp.maximum(x, 0.0) - size * tail


def attend(q, k, v, bias):
    nq = q.shape[0]
    lane_head = lax.broadcasted_iota(jnp.int32, (1, GROUP), 1) // HEAD
    stacked = jnp.concatenate(
        [q * (lane_head == h).astype(BF16) for h in range(8)], axis=0
    )
    scores = lax.dot_general(k, stacked, (((1,), (1,)), ((), ())), preferred_element_type=F32)
    if bias is not None:
        scores = scores + bias
    expo = jnp.exp2((scores - jnp.max(scores, 0, keepdims=True)) * EXP_SCALE)
    weights = (expo * (1.0 / jnp.sum(expo, 0, keepdims=True))).astype(BF16)
    full = lax.dot_general(weights, v, (((0,), (0,)), ((), ())), preferred_element_type=F32)
    out = full[:nq]
    for h in range(1, 8):
        out = jnp.where(lane_head == h, full[h * nq : (h + 1) * nq], out)
    return out


def attend_tile(qkv, width, biases):
    both, low, high = biases
    rounded = qkv.astype(BF16)
    groups = []
    for g in range(width // GROUP):
        at = [slice(part * width + g * GROUP, part * width + (g + 1) * GROUP) for part in range(3)]
        pair = attend(*[rounded[:144, s] for s in at], both)
        third = attend(
            rounded[144:224, at[0]],
            qkv[144:216, at[1]].astype(BF16),
            qkv[144:216, at[2]].astype(BF16),
            low,
        )
        fourth = attend(
            rounded[208:288, at[0]],
            qkv[216:288, at[1]].astype(BF16),
            qkv[216:288, at[2]].astype(BF16),
            high,
        )
        groups.append(jnp.concatenate([pair, third[:72], fourth[8:]], axis=0).astype(BF16))
    return jnp.concatenate(groups, axis=1)


def fill_biases(sides, biases):
    edge = lax.axis_index("lat") == lax.axis_size("lat") - 1
    large = jnp.where(edge, 5e29, 0.0).astype(F32)
    for side, bias in zip(sides, biases):
        keys = lax.broadcasted_iota(jnp.int32, (bias.shape[0], 1), 0)
        half = jnp.where(keys >= 72, keys - 72, keys) < 36
        bias[...] = (jnp.where(half, 1.0, -1.0) * side[...] - 1.0) * large


BIAS_SCRATCH = [
    pltpu.VMEM((144, 1152), F32),
    pltpu.VMEM((72, 640), F32),
    pltpu.VMEM((72, 640), F32),
]


def run(body, outs, ins, scratch=(), flops=0, limit=40):
    names, out_names = list(ins), list(outs)

    def kernel(*refs):
        body(
            dict(zip(names, refs)),
            dict(zip(out_names, refs[len(names) :])),
            refs[len(names) + len(out_names) :],
        )

    size = sum(math.prod(a.shape) * a.dtype.itemsize for a in ins.values())
    results = pl.pallas_call(
        kernel,
        out_shape=[jax.ShapeDtypeStruct(shape, BF16) for shape in outs.values()],
        in_specs=[pl.BlockSpec(memory_space=pltpu.VMEM)] * len(names),
        out_specs=[pl.BlockSpec(memory_space=pltpu.VMEM)] * len(out_names),
        scratch_shapes=list(scratch),
        compiler_params=pltpu.CompilerParams(vmem_limit_bytes=limit * MIB),
        cost_estimate=pl.CostEstimate(flops=flops, bytes_accessed=size, transcendentals=0),
    )(*ins.values())
    return dict(zip(out_names, results))


def const(table):
    return jnp.asarray(table, BF16)


def split_first(x):
    tables = first_send_tables()

    def body(ins, outs, _):
        for name in PIECE_ROWS:
            for level in range(4):
                outs[name][level] = dot(ins["t_" + name][...], ins["x"][level]).astype(BF16)

    return run(
        body,
        {name: (4, rows, 512) for name, rows in PIECE_ROWS.items()},
        {"x": x} | {"t_" + name: const(table) for name, table in tables.items()},
        limit=16,
    )


def fine_quads(quads, sources, weights, blocks, emit):
    tables = {quad: window_tables(quad) for quad in quads}
    needed = sorted({name for quad in quads for name in tables[quad]})
    ins = {name: sources[name] for name in needed} | weights
    for quad in quads:
        for name, table in tables[quad].items():
            ins["w", quad, name] = const(table)
    masked = any(quad[0] == 1 for quad in quads)
    if masked:
        for at, row in enumerate(side_rows()):
            ins["side", at] = jnp.asarray(row)
    outs = {quad: (4, 72, 512) for quad in quads}
    sends = {}
    if emit:
        for quad in QUADS:
            sends[quad] = second_send_tables(quad)
            for name, table in sends[quad].items():
                ins["s", quad, name] = const(table)
            if quad in blocks and sends[quad]:
                ins["block", quad] = blocks[quad]
        outs |= {name: (4, rows, 512) for name, rows in PIECE_ROWS.items()}

    def body(refs, outs, biases):
        if masked:
            fill_biases([refs["side", at] for at in range(3)], biases)
        for quad in quads:
            levels = []
            for level in ORDER:
                total = None
                for name in tables[quad]:
                    term = dot(refs["w", quad, name][...], refs[name][level])
                    total = term if total is None else total + term
                levels.append(total)
            tokens = jnp.concatenate(levels, axis=0)
            qkv = dot(normalize(tokens).astype(BF16), refs["qkv"][...])
            use = [bias[...] for bias in biases] if quad[0] == 1 else [None] * 3
            mixed = attend_tile(qkv, 512, use)
            hidden = (tokens + dot(mixed, refs["out"][...])).astype(BF16).astype(F32)
            normed = normalize(hidden).astype(BF16)
            total = hidden
            for at in range(0, 2048, 512):
                inner = gelu(dot(normed, refs["up"][:, at : at + 512])).astype(BF16)
                total = total + dot(inner, refs["down"][at : at + 512, :])
            for place, level in enumerate(ORDER):
                outs[quad][level] = total[place * 72 : place * 72 + 72].astype(BF16)
        if emit:
            for name in PIECE_ROWS:
                for level in range(4):
                    total = None
                    for quad in QUADS:
                        if name in sends[quad]:
                            block = outs[quad] if quad in outs else refs["block", quad]
                            term = dot(refs["s", quad, name][...], block[level])
                            total = term if total is None else total + term
                    outs[name][level] = total.astype(BF16)

    return run(
        body, outs, ins, BIAS_SCRATCH if masked else (), flops=len(quads) * 2_500_000_000
    )


def coarse(blocks, pieces, merge, qkv_weight, out_weight):
    sources = blocks | pieces
    tables = pair_tables()
    ins = {"merge": merge, "qkv": qkv_weight, "out": out_weight, "last": const(last_send_table())}
    for name, table in tables.items():
        ins["src", name] = sources[name]
        ins["t", name] = const(table)
    for at, row in enumerate(side_rows()):
        ins["side", at] = jnp.asarray(row)

    def body(refs, outs, biases):
        fill_biases([refs["side", at] for at in range(3)], biases)
        rows = []
        for level in ORDER:
            total = None
            for name in tables:
                term = dot(refs["t", name][...], refs["src", name][level])
                total = term if total is None else total + term
            pairs = jnp.concatenate([total[72 * at : 72 * at + 72] for at in range(4)], axis=1)
            rows.append(normalize(pairs))
        pairs = jnp.concatenate(rows, axis=0).astype(BF16)
        merged = dot(pairs, refs["merge"][...]).astype(BF16).astype(F32)
        qkv = dot(normalize(merged).astype(BF16), refs["qkv"][...])
        mixed = attend_tile(qkv, 1024, [bias[...] for bias in biases])
        result = (merged + dot(mixed, refs["out"][...])).astype(BF16)
        parts = dot(refs["last"][...], result)
        for part in range(4):
            outs[part][...] = parts[part * 72 : part * 72 + 72].astype(BF16)

    return run(
        body, {part: (72, 1024) for part in range(4)}, ins, BIAS_SCRATCH, flops=5_000_000_000
    )


def assemble(parts):
    def body(refs, outs, _):
        total = None
        for part in range(4):
            term = dot(refs["t"][part], refs[part][...])
            total = term if total is None else total + term
        for level in range(4):
            for row in range(6):
                at = (level * 6 + row) * 16
                outs["out"][level, row] = total[at : at + 12].astype(BF16)

    return run(
        body,
        {"out": (4, 6, 12, 1024)},
        dict(enumerate(parts)) | {"t": const(last_tables())},
        limit=16,
    )["out"]


def receive(array, lat, lon):
    rows, cols = lax.axis_size("lat"), lax.axis_size("lon")
    pairs = [
        (((a + lat) % rows) * cols + (b + lon) % cols, a * cols + b)
        for a in range(rows)
        for b in range(cols)
    ]
    return lax.ppermute(array, ("lat", "lon"), pairs)


def shift(pieces):
    return {
        "lon": receive(pieces["lon"], 0, 1),
        "lat": receive(pieces["lat"], 1, 0),
        "both": receive(pieces["both"], 1, 1),
    }


def shards(fine, fine_qkv, fine_out, fine_up, fine_down, merge_weight, coarse_qkv, coarse_out):
    weights = {"qkv": fine_qkv, "out": fine_out, "up": fine_up, "down": fine_down}
    x = fine.reshape(4, 288, 512)
    sources = {"own": x} | shift(split_first(x))
    blocks = fine_quads(QUADS[:1], sources, weights, {}, False)
    second = fine_quads(QUADS[1:3], sources, weights, blocks, True)
    pieces = shift({name: second[name] for name in PIECE_ROWS})
    blocks |= {quad: second[quad] for quad in QUADS[1:3]}
    blocks |= fine_quads(QUADS[3:], sources, weights, {}, False)
    parts = coarse(blocks, pieces, merge_weight, coarse_qkv, coarse_out)
    moved = [parts[0], receive(parts[1], 0, -1), receive(parts[2], -1, 0), receive(parts[3], -1, -1)]
    return assemble(moved)


def solution(mesh):
    in_specs = (P(None, "lat", "lon", None), P(), P(), P(), P(), P(), P(), P())
    out_specs = P(None, "lat", "lon", None)
    return jax.shard_map(shards, mesh=mesh, in_specs=in_specs, out_specs=out_specs, check_vma=False)
```

```python
import functools
import math

import jax
import jax.numpy as jnp
import numpy as np
from jax import lax
from jax.experimental import pallas as pl
from jax.experimental.pallas import tpu as pltpu
from jax.sharding import PartitionSpec as P

F32 = jnp.float32
BF16 = jnp.bfloat16
HEAD = 32
GROUP = 256
ORDER = (1, 2, 3, 0)
QUADS = ((0, 0), (0, 1), (1, 0), (1, 1))
EXP_SCALE = HEAD ** -0.5 * math.log2(math.e)
MIB = 1024 * 1024


def piece_of(i, j):
    if i >= 3 and j < 6:
        return "lon", (i - 3) * 6 + j
    if i < 3 and j >= 6:
        return "lat", i * 18 + j - 6
    if i < 3 and j < 6:
        return "both", i * 6 + j
    return None, 0


def source_of(i, j):
    i, j = i + 3, j + 6
    if i < 12 and j < 24:
        return "own", (i, j)
    return piece_of(i - 12 if i >= 12 else i, j - 24 if j >= 24 else j)


PIECE_ROWS = {"lon": 56, "lat": 56, "both": 24}


def first_send_tables():
    table, start = np.zeros((136, 288), np.float32), 0
    for name, rows in PIECE_ROWS.items():
        for i in range(12):
            for j in range(24):
                piece, at = piece_of(i, j)
                if piece == name:
                    table[start + at, i * 24 + j] = 1
        start += rows
    return table


OWN_ROWS = {"own0": 64, "own1": 144, "own2": 208}


def window_tables(quad):
    tables = {}
    for r in range(6):
        for c in range(12):
            name, at = source_of(quad[0] * 6 + r, quad[1] * 12 + c)
            if name == "own":
                row = at[0] * 24 + at[1]
                name = "own2" if quad[0] == 1 else "own1" if row >= 144 else "own0"
                at = row - OWN_ROWS[name]
            tables.setdefault(name, np.zeros((80, 80), np.float32))[r * 12 + c, at] = 1
    return tables


def second_send_tables(quad):
    tables = {}
    for r in range(6):
        for c in range(12):
            name, at = piece_of(quad[0] * 6 + r, quad[1] * 12 + c)
            if name is not None:
                tables.setdefault(name, np.zeros((80, 80), np.float32))[at, r * 12 + c] = 1
    return tables


def pair_tables():
    names = list(QUADS) + list(PIECE_ROWS)
    tables = np.zeros((7, 288, 72), np.float32)
    for i in range(12):
        for j in range(24):
            to = ((i % 2) * 2 + j % 2) * 72 + (i // 2) * 12 + j // 2
            name, at = source_of(i, j)
            if name == "own":
                name, at = (at[0] // 6, at[1] // 12), (at[0] % 6) * 12 + at[1] % 12
            tables[names.index(name), to, at] = 1
    return tables


def last_send_table():
    table = np.zeros((3, 288, 96), np.float32)
    for place, level in enumerate(ORDER):
        for i in range(6):
            for j in range(12):
                part = (i // 3) * 2 + j // 6
                to, at = part * 72 + level * 18 + (i % 3) * 6 + j % 6, place * 72 + i * 12 + j
                table[at // 96, to, at % 96] = 1
    return table


def last_tables():
    tables = np.zeros((4, 288, 72), np.float32)
    for part in range(4):
        for level in range(4):
            for i in range(3):
                for j in range(6):
                    row = i + 3 if part // 2 == 0 else i
                    col = j + 6 if part % 2 == 0 else j
                    tables[part, (row * 12 + col) * 4 + level, level * 18 + i * 6 + j] = 1
    return tables


def dot(a, b):
    return jnp.dot(a, b, preferred_element_type=F32)


def normalize(values):
    center = values - jnp.mean(values, -1, keepdims=True)
    spread = jnp.mean(center * center, -1, keepdims=True)
    return center * lax.rsqrt(spread + 1e-05)


def gelu(x):
    return 0.5 * x * (1.0 + lax.erf(x * 0.5**0.5))


def attend(q, k, v, bias):
    nq = q.shape[0]
    lane_head = lax.broadcasted_iota(jnp.int32, (1, GROUP), 1) // HEAD
    stacked = jnp.concatenate(
        [q * (lane_head == h).astype(BF16) for h in range(8)], axis=0
    )
    scores = lax.dot_general(k, stacked, (((1,), (1,)), ((), ())), preferred_element_type=F32)
    if bias is not None:
        scores = scores + bias
    expo = jnp.exp2((scores - jnp.max(scores, 0, keepdims=True)) * EXP_SCALE)
    weights = (expo * (1.0 / jnp.sum(expo, 0, keepdims=True))).astype(BF16)
    full = lax.dot_general(weights, v, (((0,), (0,)), ((), ())), preferred_element_type=F32)
    out = full[:nq]
    for h in range(1, 8):
        out = jnp.where(lane_head == h, full[h * nq : (h + 1) * nq], out)
    return out


def attend_tile(qkv, width, biases):
    both, low, high = biases
    rounded = qkv.astype(BF16)
    groups = []
    for g in range(width // GROUP):
        at = [slice(part * width + g * GROUP, part * width + (g + 1) * GROUP) for part in range(3)]
        pair = attend(*[rounded[:144, s] for s in at], both)
        third = attend(
            rounded[144:224, at[0]],
            qkv[144:216, at[1]].astype(BF16),
            qkv[144:216, at[2]].astype(BF16),
            low,
        )
        fourth = attend(
            rounded[208:288, at[0]],
            qkv[216:288, at[1]].astype(BF16),
            qkv[216:288, at[2]].astype(BF16),
            high,
        )
        groups.append(jnp.concatenate([pair, third[:72], fourth[8:]], axis=0).astype(BF16))
    return jnp.concatenate(groups, axis=1)


def fill_biases(biases):
    edge = lax.axis_index("lat") == lax.axis_size("lat") - 1
    large = jnp.where(edge, 5e29, 0.0).astype(F32)
    for bias, (start, period) in zip(biases, ((0, 144), (0, 80), (8, 80))):
        query = lax.rem(lax.broadcasted_iota(jnp.int32, (1, bias.shape[1]), 1), period) - start
        keys = lax.broadcasted_iota(jnp.int32, (bias.shape[0], 1), 0)
        sides = [
            jnp.where(jnp.where(place >= 72, place - 72, place) < 36, 1.0, -1.0)
            for place in (keys, query)
        ]
        bias[...] = (sides[0] * sides[1] - 1.0) * large


BIAS_SCRATCH = [
    pltpu.VMEM((144, 1152), F32),
    pltpu.VMEM((72, 640), F32),
    pltpu.VMEM((72, 640), F32),
]


def run(body, outs, ins, scratch=(), flops=0, limit=32):
    names, out_names = list(ins), list(outs)

    def kernel(*refs):
        first, last = len(names), len(names) + len(out_names)
        body(dict(zip(names, refs)), dict(zip(out_names, refs[first:last])), refs[last:])

    size = sum(math.prod(array.shape) * 2 for array in ins.values())
    results = pl.pallas_call(
        kernel,
        out_shape=[jax.ShapeDtypeStruct(shape, BF16) for shape in outs.values()],
        in_specs=[pl.BlockSpec(memory_space=pltpu.VMEM)] * len(names),
        out_specs=[pl.BlockSpec(memory_space=pltpu.VMEM)] * len(out_names),
        scratch_shapes=list(scratch),
        compiler_params=pltpu.CompilerParams(vmem_limit_bytes=limit * MIB),
        cost_estimate=pl.CostEstimate(flops=flops, bytes_accessed=size, transcendentals=0),
    )(*ins.values())
    return dict(zip(out_names, results))


def const(table):
    return jnp.asarray(table, BF16)


def split_first(x):
    def body(refs, outs, _):
        for level in range(4):
            rows = dot(refs["table"][...], refs["x"][level])
            start = 0
            for name, count in PIECE_ROWS.items():
                outs[name][level] = rows[start : start + count].astype(BF16)
                start += count

    return run(
        body,
        {name: (4, rows, 512) for name, rows in PIECE_ROWS.items()},
        {"table": const(first_send_tables()), "x": x},
        flops=10_000_000_000,
        limit=8,
    )


CHUNK = 512


def fine_quads(quads, sources, weights, blocks, emit):
    tables = {quad: window_tables(quad) for quad in quads}
    needed = sorted({name for quad in quads for name in tables[quad]})
    ins = {name: sources[name] for name in needed if name in PIECE_ROWS}
    ins |= {"own": sources["own"]} | weights
    stack, place = [], {}
    for quad in quads:
        for name, table in tables[quad].items():
            place[quad, name] = len(stack)
            stack.append(table)
    masked = any(quad[0] == 1 for quad in quads)
    outs = {quad: (4, 72, 512) for quad in quads}
    sends = {}
    if emit:
        for quad in QUADS:
            sends[quad] = second_send_tables(quad)
            for name, table in sends[quad].items():
                place["send", quad, name] = len(stack)
                stack.append(table)
            if quad in blocks and sends[quad]:
                ins["block", quad] = blocks[quad]
        outs |= {name: (4, rows, 512) for name, rows in PIECE_ROWS.items()}
    ins["table"] = const(np.stack(stack))

    def body(refs, outs, biases):
        if masked:
            fill_biases(biases)
        for quad in quads:
            levels = []
            for level in ORDER:
                total = None
                for name in tables[quad]:
                    if name in PIECE_ROWS:
                        source = refs[name][level]
                    else:
                        source = refs["own"][level, OWN_ROWS[name] : OWN_ROWS[name] + 80, :]
                    term = dot(refs["table"][place[quad, name], :72, : source.shape[0]], source)
                    total = term if total is None else total + term
                levels.append(total)
            tokens = jnp.concatenate(levels, axis=0)
            qkv = dot(normalize(tokens).astype(BF16), refs["qkv"][...])
            use = [bias[...] for bias in biases] if quad[0] == 1 else [None] * 3
            mixed = attend_tile(qkv, 512, use)
            hidden = (tokens + dot(mixed, refs["out"][...])).astype(BF16).astype(F32)
            normed = normalize(hidden).astype(BF16)
            total = hidden
            for at in range(0, 2048, CHUNK):
                inner = gelu(dot(normed, refs["up"][:, at : at + CHUNK])).astype(BF16)
                total = total + dot(inner, refs["down"][at : at + CHUNK, :])
            for at, level in enumerate(ORDER):
                outs[quad][level] = total[at * 72 : at * 72 + 72].astype(BF16)
        if emit:
            for name, rows in PIECE_ROWS.items():
                for level in range(4):
                    total = None
                    for quad in QUADS:
                        if name in sends[quad]:
                            block = outs[quad] if quad in outs else refs["block", quad]
                            table = refs["table"][place["send", quad, name], :rows, :72]
                            term = dot(table, block[level])
                            total = term if total is None else total + term
                    outs[name][level] = total.astype(BF16)

    return run(
        body, outs, ins, BIAS_SCRATCH if masked else (), flops=len(quads) * 2_500_000_000
    )


def coarse(blocks, pieces, merge, qkv_weight, out_weight):
    ins = {"table": const(pair_tables())}
    ins |= {"src%d" % at: array for at, array in enumerate([blocks[quad] for quad in QUADS])}
    ins |= {"src%d" % (4 + at): pieces[name] for at, name in enumerate(PIECE_ROWS)}
    ins |= {"merge": merge, "qkv": qkv_weight, "out": out_weight}
    ins |= {"last": const(last_send_table())}

    def body(refs, outs, biases):
        fill_biases(biases)
        rows = []
        for level in ORDER:
            total = None
            for at in range(7):
                source = refs["src%d" % at][level]
                term = dot(refs["table"][at, :, : source.shape[0]], source)
                total = term if total is None else total + term
            pairs = jnp.concatenate([total[72 * at : 72 * at + 72] for at in range(4)], axis=1)
            rows.append(normalize(pairs))
        pairs = jnp.concatenate(rows, axis=0).astype(BF16)
        merged = dot(pairs, refs["merge"][...]).astype(BF16).astype(F32)
        qkv = dot(normalize(merged).astype(BF16), refs["qkv"][...])
        mixed = attend_tile(qkv, 1024, [bias[...] for bias in biases])
        result = (merged + dot(mixed, refs["out"][...])).astype(BF16)
        parts = sum(dot(refs["last"][at], result[96 * at : 96 * at + 96]) for at in range(3))
        for part in range(4):
            outs[part][...] = parts[part * 72 : part * 72 + 72].astype(BF16)

    return run(
        body,
        {part: (72, 1024) for part in range(4)},
        ins,
        BIAS_SCRATCH,
        flops=5_000_000_000,
    )


def assemble(parts):
    def body(refs, outs, _):
        total = None
        for part in range(4):
            term = dot(refs["table"][part], refs[part][...])
            total = term if total is None else total + term
        for row in range(6):
            for col in range(12):
                at = (row * 12 + col) * 4
                outs["out"][row, col] = total[at : at + 4].astype(BF16)

    result = run(
        body,
        {"out": (6, 12, 4, 1024)},
        {"table": const(last_tables())} | dict(enumerate(parts)),
        limit=8,
    )["out"]
    return result.transpose(2, 0, 1, 3)


def receive(array, lat, lon):
    rows, cols = lax.axis_size("lat"), lax.axis_size("lon")
    pairs = [
        (((a + lat) % rows) * cols + (b + lon) % cols, a * cols + b)
        for a in range(rows)
        for b in range(cols)
    ]
    return lax.ppermute(array, ("lat", "lon"), pairs)


def shift(pieces):
    return {
        "lon": receive(pieces["lon"], 0, 1),
        "lat": receive(pieces["lat"], 1, 0),
        "both": receive(pieces["both"], 1, 1),
    }


def shards(fine, fine_qkv, fine_out, fine_up, fine_down, merge_weight, coarse_qkv, coarse_out):
    weights = {"qkv": fine_qkv, "out": fine_out, "up": fine_up, "down": fine_down}
    x = fine.reshape(4, 288, 512)
    sources = {"own": x} | shift(split_first(x))
    blocks = fine_quads(QUADS[:1], sources, weights, {}, False)
    second = fine_quads(QUADS[1:3], sources, weights, blocks, True)
    pieces = shift({name: second[name] for name in PIECE_ROWS})
    blocks |= {quad: second[quad] for quad in QUADS[1:3]}
    blocks |= fine_quads(QUADS[3:], sources, weights, {}, False)
    parts = coarse(blocks, pieces, merge_weight, coarse_qkv, coarse_out)
    moved = [parts[0], receive(parts[1], 0, -1), receive(parts[2], -1, 0), receive(parts[3], -1, -1)]
    return assemble(moved)


def solution(mesh):
    in_specs = (P(None, "lat", "lon", None), P(), P(), P(), P(), P(), P(), P())
    out_specs = P(None, "lat", "lon", None)
    return jax.shard_map(shards, mesh=mesh, in_specs=in_specs, out_specs=out_specs, check_vma=False)
```

```python
import functools
import math

import jax
import jax.numpy as jnp
import numpy as np
from jax import lax
from jax.experimental import pallas as pl
from jax.experimental.pallas import tpu as pltpu
from jax.sharding import PartitionSpec as P

F32 = jnp.float32
BF16 = jnp.bfloat16
HEAD = 32
GROUP = 256
ORDER = (1, 2, 3, 0)
QUADS = ((0, 0), (0, 1), (1, 0), (1, 1))
EXP_SCALE = HEAD ** -0.5 * math.log2(math.e)
MIB = 1024 * 1024


def piece_of(i, j):
    if i >= 3 and j < 6:
        return "lon", (i - 3) * 6 + j
    if i < 3 and j >= 6:
        return "lat", i * 18 + j - 6
    if i < 3 and j < 6:
        return "both", i * 6 + j
    return None, 0


def source_of(i, j):
    i, j = i + 3, j + 6
    if i < 12 and j < 24:
        return "own", (i, j)
    return piece_of(i - 12 if i >= 12 else i, j - 24 if j >= 24 else j)


PIECE_ROWS = {"lon": 56, "lat": 56, "both": 24}


def first_send_table():
    row = lax.broadcasted_iota(jnp.int32, (136, 1), 0).astype(F32)

    def at(start, width, first_row, first_col):
        place = row - start
        line = jnp.floor((place + 0.5) / width)
        return (line + first_row) * 24 + (place - line * width) + first_col

    source = jnp.where(row < 56, at(0, 6, 3, 0), jnp.where(row < 112, at(56, 18, 0, 6), at(112, 6, 0, 0)))
    lane = lax.broadcasted_iota(jnp.int32, (136, 288), 1).astype(F32)
    return (lane == source).astype(F32).astype(BF16)


OWN_ROWS = ((64, 224), (208, 288))
GATHER = (
    {"own": 0, "lon": 160},
    {"own": 0, "lon": 80, "lat": 144, "both": 208},
)


def window_table(quad):
    table, used = np.zeros((2, 80, 128), np.float32), set()
    for r in range(6):
        for c in range(12):
            name, at = source_of(quad[0] * 6 + r, quad[1] * 12 + c)
            used.add(name)
            if name == "own":
                at = at[0] * 24 + at[1] - OWN_ROWS[quad[0]][0]
            at += GATHER[quad[0]][name]
            table[at // 128, r * 12 + c, at % 128] = 1
    return table, sorted(used)


def second_send_tables(quad):
    tables = {}
    for r in range(6):
        for c in range(12):
            name, at = piece_of(quad[0] * 6 + r, quad[1] * 12 + c)
            if name is not None:
                tables.setdefault(name, np.zeros((80, 128), np.float32))[at, r * 12 + c] = 1
    return tables


PAIR_GATHER = {quad: 80 * at for at, quad in enumerate(QUADS)}
PAIR_GATHER |= {"lon": 320, "lat": 384, "both": 448}


def pair_tables():
    table = np.zeros((4, 288, 128), np.float32)
    for i in range(12):
        for j in range(24):
            to = ((i % 2) * 2 + j % 2) * 72 + (i // 2) * 12 + j // 2
            name, at = source_of(i, j)
            if name == "own":
                name, at = (at[0] // 6, at[1] // 12), (at[0] % 6) * 12 + at[1] % 12
            at += PAIR_GATHER[name]
            table[at // 128, to, at % 128] = 1
    return table


def last_send_table():
    table = np.zeros((3, 288, 96), np.float32)
    for place, level in enumerate(ORDER):
        for i in range(6):
            for j in range(12):
                part = (i // 3) * 2 + j // 6
                to, at = part * 72 + ((i % 3) * 6 + j % 6) * 4 + level, place * 72 + i * 12 + j
                table[at // 96, to, at % 96] = 1
    return table


def dot(a, b):
    return jnp.dot(a, b, preferred_element_type=F32)


def normalize(values):
    center = values - jnp.mean(values, -1, keepdims=True)
    spread = jnp.mean(center * center, -1, keepdims=True)
    return center * lax.rsqrt(spread + 1e-05)


def gelu(x):
    return 0.5 * x * (1.0 + lax.erf(x * 0.5**0.5))


def attend(q, k, v, bias, first):
    lane_head = lax.broadcasted_iota(jnp.int32, (1, GROUP), 1) // HEAD
    stacked = jnp.concatenate(
        [q * (lane_head == h).astype(BF16) for h in range(8)], axis=0
    )
    scores = lax.dot_general(k, stacked, (((1,), (1,)), ((), ())), preferred_element_type=F32)
    if first is not None:
        scores = jnp.where(first, scores[:72], scores[72:])
    if bias is not None:
        scores = scores + bias[: scores.shape[0]]
    expo = jnp.exp2((scores - jnp.max(scores, 0, keepdims=True)) * EXP_SCALE)
    weights = expo * (1.0 / jnp.sum(expo, 0, keepdims=True))
    if first is not None:
        parts = [jnp.where(first, weights, 0.0), jnp.where(first, 0.0, weights)]
        weights = jnp.concatenate(parts, axis=0)
    full = lax.dot_general(
        weights.astype(BF16), v, (((0,), (0,)), ((), ())), preferred_element_type=F32
    )
    out = full[:144]
    for h in range(1, 8):
        out = jnp.where(lane_head == h, full[h * 144 : h * 144 + 144], out)
    return out


def attend_tile(qkv, width, bias):
    lane = lax.broadcasted_iota(jnp.int32, (1, 1152), 1)
    first = lax.rem(lane, 144) < 72
    groups = []
    for g in range(width // GROUP):
        at = [slice(part * width + g * GROUP, part * width + (g + 1) * GROUP) for part in range(3)]
        pair = attend(*[qkv[:144, s] for s in at], bias, None)
        alone = attend(*[qkv[144:, s] for s in at], bias, first)
        groups.append(jnp.concatenate([pair, alone], axis=0).astype(BF16))
    return jnp.concatenate(groups, axis=1)


def fill_bias(bias):
    edge = lax.axis_index("lat") == lax.axis_size("lat") - 1
    large = jnp.where(edge, 5e29, 0.0).astype(F32)
    query = lax.rem(lax.broadcasted_iota(jnp.int32, (1, 1152), 1), 144)
    keys = lax.broadcasted_iota(jnp.int32, (144, 1), 0)
    sides = [
        jnp.where(jnp.where(place >= 72, place - 72, place) < 36, 1.0, -1.0)
        for place in (keys, query)
    ]
    bias[...] = (sides[0] * sides[1] - 1.0) * large


BIAS = pltpu.VMEM((144, 1152), F32)


def run(body, outs, ins, scratch=(), flops=0, limit=32):
    names, out_names = list(ins), list(outs)

    def kernel(*refs):
        first, last = len(names), len(names) + len(out_names)
        body(dict(zip(names, refs)), dict(zip(out_names, refs[first:last])), refs[last:])

    size = sum(math.prod(array.shape) * 2 for array in ins.values())
    results = pl.pallas_call(
        kernel,
        out_shape=[jax.ShapeDtypeStruct(shape, BF16) for shape in outs.values()],
        in_specs=[pl.BlockSpec(memory_space=pltpu.VMEM)] * len(names),
        out_specs=[pl.BlockSpec(memory_space=pltpu.VMEM)] * len(out_names),
        scratch_shapes=list(scratch),
        compiler_params=pltpu.CompilerParams(vmem_limit_bytes=limit * MIB),
        cost_estimate=pl.CostEstimate(flops=flops, bytes_accessed=size, transcendentals=0),
    )(*ins.values())
    return dict(zip(out_names, results))


def const(table):
    return jnp.asarray(table, BF16)


def split_first(x):
    def body(refs, outs, _):
        table = first_send_table()
        for level in range(4):
            rows = dot(table, refs["x"][level])
            start = 0
            for name, count in PIECE_ROWS.items():
                outs[name][level] = rows[start : start + count].astype(BF16)
                start += count

    return run(
        body,
        {name: (4, rows, 512) for name, rows in PIECE_ROWS.items()},
        {"x": x},
        flops=10_000_000_000,
        limit=8,
    )


CHUNK = 1024


def fine_quads(quads, sources, weights, blocks, emit):
    tables = {quad: window_table(quad) for quad in quads}
    needed = sorted({name for quad in quads for name in tables[quad][1]})
    ins = {name: sources[name] for name in needed} | weights
    stack, place = [], {}
    for quad in quads:
        place[quad] = len(stack)
        stack += list(tables[quad][0])
    masked = any(quad[0] == 1 for quad in quads)
    outs = {quad: (4, 72, 512) for quad in quads}
    sends = {}
    if emit:
        for quad in QUADS:
            sends[quad] = second_send_tables(quad)
            for name, table in sends[quad].items():
                place["send", quad, name] = len(stack)
                stack.append(table)
            if quad in blocks and sends[quad]:
                ins["block", quad] = blocks[quad]
        outs |= {name: (4, rows, 512) for name, rows in PIECE_ROWS.items()}
    ins["table"] = const(np.stack(stack))

    def body(refs, outs, scratch):
        gathered = scratch[0]
        gathered[...] = jnp.zeros_like(gathered)
        if masked:
            fill_bias(scratch[1])
        for at, quad in enumerate(quads):
            table = [refs["table"][place[quad] + part, :72, :] for part in range(2)]
            table = jnp.concatenate(table, axis=1)
            levels = []
            for level in ORDER:
                for name in tables[quad][1]:
                    rows = slice(*OWN_ROWS[quad[0]]) if name == "own" else slice(None)
                    source = refs[name][level, rows, :]
                    start = GATHER[quad[0]][name]
                    gathered[at * 4 + level, start : start + source.shape[0], :] = source
                levels.append(dot(table, gathered[at * 4 + level]))
            tokens = jnp.concatenate(levels, axis=0)
            qkv = dot(normalize(tokens).astype(BF16), refs["qkv"][...]).astype(BF16)
            mixed = attend_tile(qkv, 512, scratch[1] if quad[0] == 1 else None)
            hidden = (tokens + dot(mixed, refs["out"][...])).astype(BF16).astype(F32)
            normed = normalize(hidden).astype(BF16)
            total = hidden
            for at in range(0, 2048, CHUNK):
                inner = gelu(dot(normed, refs["up"][:, at : at + CHUNK])).astype(BF16)
                total = total + dot(inner, refs["down"][at : at + CHUNK, :])
            for at, level in enumerate(ORDER):
                outs[quad][level] = total[at * 72 : at * 72 + 72].astype(BF16)
        if emit:
            for name, rows in PIECE_ROWS.items():
                for level in range(4):
                    total = None
                    for quad in QUADS:
                        if name in sends[quad]:
                            block = outs[quad] if quad in outs else refs["block", quad]
                            table = refs["table"][place["send", quad, name], :rows, :72]
                            term = dot(table, block[level])
                            total = term if total is None else total + term
                    outs[name][level] = total.astype(BF16)

    return run(
        body,
        outs,
        ins,
        [pltpu.VMEM((4 * len(quads), 256, 512), BF16)] + ([BIAS] if masked else []),
        flops=len(quads) * 2_500_000_000,
    )


def coarse(blocks, pieces, merge, qkv_weight, out_weight):
    sources = {("from", quad): blocks[quad] for quad in QUADS}
    sources |= {("from", name): pieces[name] for name in PIECE_ROWS}
    ins = sources | {"table": const(pair_tables()), "last": const(last_send_table())}
    ins |= {"merge": merge, "qkv": qkv_weight, "out": out_weight}

    def body(refs, outs, scratch):
        gathered, bias = scratch
        gathered[...] = jnp.zeros_like(gathered)
        fill_bias(bias)
        table = jnp.concatenate([refs["table"][at] for at in range(4)], axis=1)
        rows = []
        for level in ORDER:
            for name, start in PAIR_GATHER.items():
                source = refs["from", name][level]
                gathered[level, start : start + source.shape[0], :] = source
            total = dot(table, gathered[level])
            pairs = jnp.concatenate([total[72 * at : 72 * at + 72] for at in range(4)], axis=1)
            rows.append(normalize(pairs))
        pairs = jnp.concatenate(rows, axis=0).astype(BF16)
        merged = dot(pairs, refs["merge"][...]).astype(BF16).astype(F32)
        qkv = dot(normalize(merged).astype(BF16), refs["qkv"][...]).astype(BF16)
        mixed = attend_tile(qkv, 1024, bias)
        result = (merged + dot(mixed, refs["out"][...])).astype(BF16)
        parts = sum(dot(refs["last"][at], result[96 * at : 96 * at + 96]) for at in range(3))
        for part in range(4):
            for at in range(18):
                start = part * 72 + at * 4
                outs[part][at // 6, at % 6] = parts[start : start + 4].astype(BF16)

    return run(
        body,
        {part: (3, 6, 4, 1024) for part in range(4)},
        ins,
        [pltpu.VMEM((4, 512, 512), BF16), BIAS],
        flops=5_000_000_000,
    )


def assemble(parts):
    def body(refs, outs, _):
        for at in range(4):
            row, col = (3, 0)[at // 2], (6, 0)[at % 2]
            outs["out"][row : row + 3, col : col + 6] = refs[at][...]

    result = run(body, {"out": (6, 12, 4, 1024)}, dict(enumerate(parts)), limit=8)["out"]
    return result.transpose(2, 0, 1, 3)


def receive(array, lat, lon):
    rows, cols = lax.axis_size("lat"), lax.axis_size("lon")
    pairs = [
        (((a + lat) % rows) * cols + (b + lon) % cols, a * cols + b)
        for a in range(rows)
        for b in range(cols)
    ]
    return lax.ppermute(array, ("lat", "lon"), pairs)


def shift(pieces):
    return {
        "lon": receive(pieces["lon"], 0, 1),
        "lat": receive(pieces["lat"], 1, 0),
        "both": receive(pieces["both"], 1, 1),
    }


def shards(fine, fine_qkv, fine_out, fine_up, fine_down, merge_weight, coarse_qkv, coarse_out):
    weights = {"qkv": fine_qkv, "out": fine_out, "up": fine_up, "down": fine_down}
    x = fine.reshape(4, 288, 512)
    sources = {"own": x} | shift(split_first(x))
    blocks = fine_quads(QUADS[:1], sources, weights, {}, False)
    second = fine_quads(QUADS[1:3], sources, weights, blocks, True)
    pieces = shift({name: second[name] for name in PIECE_ROWS})
    blocks |= {quad: second[quad] for quad in QUADS[1:3]}
    blocks |= fine_quads(QUADS[3:], sources, weights, {}, False)
    parts = coarse(blocks, pieces, merge_weight, coarse_qkv, coarse_out)
    moved = [parts[0], receive(parts[1], 0, -1), receive(parts[2], -1, 0), receive(parts[3], -1, -1)]
    return assemble(moved)


def solution(mesh):
    in_specs = (P(None, "lat", "lon", None), P(), P(), P(), P(), P(), P(), P())
    out_specs = P(None, "lat", "lon", None)
    return jax.shard_map(shards, mesh=mesh, in_specs=in_specs, out_specs=out_specs, check_vma=False)
```

```python
import functools
import math

import jax
import jax.numpy as jnp
import numpy as np
from jax import lax
from jax.experimental import pallas as pl
from jax.experimental.pallas import tpu as pltpu
from jax.sharding import PartitionSpec as P

F32 = jnp.float32
BF16 = jnp.bfloat16
HEAD = 32
GROUP = 256
ORDER = (1, 2, 3, 0)
QUADS = ((0, 0), (0, 1), (1, 0), (1, 1))
EXP_SCALE = HEAD ** -0.5 * math.log2(math.e)
MIB = 1024 * 1024


def piece_of(i, j):
    if i >= 3 and j < 6:
        return "lon", (i - 3) * 6 + j
    if i < 3 and j >= 6:
        return "lat", i * 18 + j - 6
    if i < 3 and j < 6:
        return "both", i * 6 + j
    return None, 0


def source_of(i, j):
    i, j = i + 3, j + 6
    if i < 12 and j < 24:
        return "own", (i, j)
    return piece_of(i - 12 if i >= 12 else i, j - 24 if j >= 24 else j)


PIECE_ROWS = {"lon": 56, "lat": 56, "both": 24}


def first_send_table():
    row = lax.broadcasted_iota(jnp.int32, (112, 1), 0).astype(F32)

    def at(start, width, first_row, first_col):
        place = row - start
        line = jnp.floor((place + 0.5) / width)
        return (line + first_row) * 24 + (place - line * width) + first_col

    source = jnp.where(row < 56, at(0, 6, 3, 0), at(56, 18, 0, 6))
    lane = lax.broadcasted_iota(jnp.int32, (112, 288), 1).astype(F32)
    return (lane == source).astype(F32).astype(BF16)


OWN_ROWS = ((64, 224), (208, 288))
GATHER = (
    {"own": 0, "lon": 160},
    {"own": 0, "lon": 80, "lat": 144, "both": 208},
)


def window_table(quad):
    table, used = np.zeros((2, 80, 128), np.float32), set()
    for r in range(6):
        for c in range(12):
            name, at = source_of(quad[0] * 6 + r, quad[1] * 12 + c)
            used.add(name)
            if name == "own":
                at = at[0] * 24 + at[1] - OWN_ROWS[quad[0]][0]
            at += GATHER[quad[0]][name]
            table[at // 128, r * 12 + c, at % 128] = 1
    return table, sorted(used)


def second_send_tables(quad):
    tables = {}
    for r in range(6):
        for c in range(12):
            name, at = piece_of(quad[0] * 6 + r, quad[1] * 12 + c)
            if name is not None:
                tables.setdefault(name, np.zeros((80, 128), np.float32))[at, r * 12 + c] = 1
    return tables


PAIR_GATHER = {quad: 80 * at for at, quad in enumerate(QUADS)}
PAIR_GATHER |= {"lon": 320, "lat": 384, "both": 448}


def pair_tables():
    table = np.zeros((4, 288, 128), np.float32)
    for i in range(12):
        for j in range(24):
            to = ((i % 2) * 2 + j % 2) * 72 + (i // 2) * 12 + j // 2
            name, at = source_of(i, j)
            if name == "own":
                name, at = (at[0] // 6, at[1] // 12), (at[0] % 6) * 12 + at[1] % 12
            at += PAIR_GATHER[name]
            table[at // 128, to, at % 128] = 1
    return table


def last_send_table():
    table = np.zeros((3, 288, 96), np.float32)
    for place, level in enumerate(ORDER):
        for i in range(6):
            for j in range(12):
                part = (i // 3) * 2 + j // 6
                to, at = part * 72 + ((i % 3) * 6 + j % 6) * 4 + level, place * 72 + i * 12 + j
                table[at // 96, to, at % 96] = 1
    return table


def dot(a, b):
    return jnp.dot(a, b, preferred_element_type=F32)


def normalize(values):
    center = values - jnp.mean(values, -1, keepdims=True)
    spread = jnp.mean(center * center, -1, keepdims=True)
    return center * lax.rsqrt(spread + 1e-05)


def gelu(x):
    return 0.5 * x * (1.0 + lax.erf(x * 0.5**0.5))


def score(q, k):
    lane_head = lax.broadcasted_iota(jnp.int32, (1, GROUP), 1) // HEAD
    stacked = jnp.concatenate(
        [q * (lane_head == h).astype(BF16) for h in range(8)], axis=0
    )
    return lax.dot_general(k, stacked, (((1,), (1,)), ((), ())), preferred_element_type=F32)


def mix(scores, v, bias, first):
    if first is not None:
        scores = jnp.where(first, scores[:72], scores[72:])
    if bias is not None:
        scores = scores + bias[: scores.shape[0]]
    expo = jnp.exp2((scores - jnp.max(scores, 0, keepdims=True)) * EXP_SCALE)
    weights = expo * (1.0 / jnp.sum(expo, 0, keepdims=True))
    if first is not None:
        parts = [jnp.where(first, weights, 0.0), jnp.where(first, 0.0, weights)]
        weights = jnp.concatenate(parts, axis=0)
    full = lax.dot_general(
        weights.astype(BF16), v, (((0,), (0,)), ((), ())), preferred_element_type=F32
    )
    lane_head = lax.broadcasted_iota(jnp.int32, (1, GROUP), 1) // HEAD
    out = full[:144]
    for h in range(1, 8):
        out = jnp.where(lane_head == h, full[h * 144 : h * 144 + 144], out)
    return out.astype(BF16)


def attend(qkv, width, biases):
    lane = lax.broadcasted_iota(jnp.int32, (1, 1152), 1)
    first = lax.rem(lane, 144) < 72
    units = []
    for at, bias in enumerate(biases):
        for g in range(width // GROUP):
            for half in range(2):
                rows = slice(at * 288 + half * 144, at * 288 + half * 144 + 144)
                lanes = [
                    slice(part * width + g * GROUP, part * width + (g + 1) * GROUP)
                    for part in range(3)
                ]
                operands = [qkv[rows, s] for s in lanes]
                units.append((at, g, half, operands, bias, first if half else None))
    outs = {}
    ready = score(*units[0][3][:2])
    for at, (tile, g, half, operands, bias, alone) in enumerate(units):
        ahead = score(*units[at + 1][3][:2]) if at + 1 < len(units) else None
        outs[tile, half, g] = mix(ready, operands[2], bias, alone)
        ready = ahead
    rows = []
    for tile in range(len(biases)):
        for half in range(2):
            row = [outs[tile, half, g] for g in range(width // GROUP)]
            rows.append(jnp.concatenate(row, axis=1))
    return jnp.concatenate(rows, axis=0)


def fill_bias(bias):
    edge = lax.axis_index("lat") == lax.axis_size("lat") - 1
    large = jnp.where(edge, 5e29, 0.0).astype(F32)
    query = lax.rem(lax.broadcasted_iota(jnp.int32, (1, 1152), 1), 144)
    keys = lax.broadcasted_iota(jnp.int32, (144, 1), 0)
    sides = [
        jnp.where(jnp.where(place >= 72, place - 72, place) < 36, 1.0, -1.0)
        for place in (keys, query)
    ]
    bias[...] = (sides[0] * sides[1] - 1.0) * large


BIAS = pltpu.VMEM((144, 1152), F32)


def run(body, outs, ins, scratch=(), flops=0, limit=32):
    names, out_names = list(ins), list(outs)

    def kernel(*refs):
        first, last = len(names), len(names) + len(out_names)
        body(dict(zip(names, refs)), dict(zip(out_names, refs[first:last])), refs[last:])

    size = sum(math.prod(array.shape) * 2 for array in ins.values())
    results = pl.pallas_call(
        kernel,
        out_shape=[jax.ShapeDtypeStruct(shape, BF16) for shape in outs.values()],
        in_specs=[pl.BlockSpec(memory_space=pltpu.VMEM)] * len(names),
        out_specs=[pl.BlockSpec(memory_space=pltpu.VMEM)] * len(out_names),
        scratch_shapes=list(scratch),
        compiler_params=pltpu.CompilerParams(vmem_limit_bytes=limit * MIB),
        cost_estimate=pl.CostEstimate(flops=flops, bytes_accessed=size, transcendentals=0),
    )(*ins.values())
    return dict(zip(out_names, results))


def const(table):
    return jnp.asarray(table, BF16)


def split_first(x):
    def body(refs, outs, _):
        table = first_send_table()
        for level in range(4):
            rows = dot(table, refs["x"][level])
            outs["lon"][level] = rows[:56].astype(BF16)
            outs["lat"][level] = rows[56:].astype(BF16)

    return run(
        body,
        {name: (4, PIECE_ROWS[name], 512) for name in ("lon", "lat")},
        {"x": x},
        flops=10_000_000_000,
        limit=8,
    )


def corner_table():
    table = np.zeros((80, 128), np.float32)
    for i in range(3):
        for j in range(6):
            table[i * 6 + j, i * 24 + j] = 1
    return table


CHUNK = 1024


def fine_quads(quads, sources, weights, blocks, emit):
    tables = {quad: window_table(quad) for quad in quads}
    needed = sorted({name for quad in quads for name in tables[quad][1]})
    ins = {name: sources[name] for name in needed} | weights
    stack, place = [], {}
    for quad in quads:
        place[quad] = len(stack)
        stack += list(tables[quad][0])
    masked = any(quad[0] == 1 for quad in quads)
    outs = {quad: (4, 72, 512) for quad in quads}
    sends = {}
    if emit:
        for quad in QUADS:
            sends[quad] = second_send_tables(quad)
            sends[quad] = {name: sends[quad][name] for name in emit if name in sends[quad]}
            for name, table in sends[quad].items():
                place["send", quad, name] = len(stack)
                stack.append(table)
            if quad in blocks and sends[quad]:
                ins["block", quad] = blocks[quad]
        outs |= {name: (8 if name == "both" else 4, PIECE_ROWS[name], 512) for name in emit}
    if "both" in emit:
        place["corner"] = len(stack)
        stack.append(corner_table())
    ins["table"] = const(np.stack(stack))

    def body(refs, outs, scratch):
        gathered = scratch[0]
        gathered[...] = jnp.zeros_like(gathered)
        if masked:
            fill_bias(scratch[1])
        levels = []
        for at, quad in enumerate(quads):
            table = [refs["table"][place[quad] + part, :72, :] for part in range(2)]
            table = jnp.concatenate(table, axis=1)
            for level in ORDER:
                for name in tables[quad][1]:
                    rows = slice(*OWN_ROWS[quad[0]]) if name == "own" else slice(None)
                    source = refs[name][level, rows, :]
                    start = GATHER[quad[0]][name]
                    gathered[at * 4 + level, start : start + source.shape[0], :] = source
                levels.append(dot(table, gathered[at * 4 + level]))
        tokens = jnp.concatenate(levels, axis=0)
        qkv = dot(normalize(tokens).astype(BF16), refs["qkv"][...]).astype(BF16)
        mixed = attend(qkv, 512, [scratch[1] if quad[0] == 1 else None for quad in quads])
        hidden = (tokens + dot(mixed, refs["out"][...])).astype(BF16).astype(F32)
        normed = normalize(hidden).astype(BF16)
        total = hidden
        for at in range(0, 2048, CHUNK):
            inner = gelu(dot(normed, refs["up"][:, at : at + CHUNK])).astype(BF16)
            total = total + dot(inner, refs["down"][at : at + CHUNK, :])
        for at, quad in enumerate(quads):
            for place_at, level in enumerate(ORDER):
                start = at * 288 + place_at * 72
                outs[quad][level] = total[start : start + 72].astype(BF16)
        for name in emit:
            rows = PIECE_ROWS[name]
            for level in range(4):
                total = None
                for quad in QUADS:
                    if name in sends[quad]:
                        block = outs[quad] if quad in outs else refs["block", quad]
                        table = refs["table"][place["send", quad, name], :rows, :72]
                        term = dot(table, block[level])
                        total = term if total is None else total + term
                if name == "both":
                    corner = dot(refs["table"][place["corner"], :24, :80], refs["own"][level, :80, :])
                    outs[name][level] = corner.astype(BF16)
                outs[name][level + (4 if name == "both" else 0)] = total.astype(BF16)

    return run(
        body,
        outs,
        ins,
        [pltpu.VMEM((4 * len(quads), 256, 512), BF16)] + ([BIAS] if masked else []),
        flops=len(quads) * 2_500_000_000,
    )


def coarse(blocks, pieces, merge, qkv_weight, out_weight):
    sources = {("from", quad): blocks[quad] for quad in QUADS}
    sources |= {("from", name): pieces[name] for name in PIECE_ROWS}
    ins = sources | {"table": const(pair_tables()), "last": const(last_send_table())}
    ins |= {"merge": merge, "qkv": qkv_weight, "out": out_weight}

    def body(refs, outs, scratch):
        gathered, bias = scratch
        gathered[...] = jnp.zeros_like(gathered)
        fill_bias(bias)
        table = jnp.concatenate([refs["table"][at] for at in range(4)], axis=1)
        rows = []
        for level in ORDER:
            for name, start in PAIR_GATHER.items():
                source = refs["from", name][level + (4 if name == "both" else 0)]
                gathered[level, start : start + source.shape[0], :] = source
            total = dot(table, gathered[level])
            pairs = jnp.concatenate([total[72 * at : 72 * at + 72] for at in range(4)], axis=1)
            rows.append(normalize(pairs))
        pairs = jnp.concatenate(rows, axis=0).astype(BF16)
        merged = dot(pairs, refs["merge"][...]).astype(BF16).astype(F32)
        qkv = dot(normalize(merged).astype(BF16), refs["qkv"][...]).astype(BF16)
        mixed = attend(qkv, 1024, [bias])
        result = (merged + dot(mixed, refs["out"][...])).astype(BF16)
        parts = sum(dot(refs["last"][at], result[96 * at : 96 * at + 96]) for at in range(3))
        for part in range(4):
            for at in range(18):
                start = part * 72 + at * 4
                outs[part][at // 6, at % 6] = parts[start : start + 4].astype(BF16)

    return run(
        body,
        {part: (3, 6, 4, 1024) for part in range(4)},
        ins,
        [pltpu.VMEM((4, 512, 512), BF16), BIAS],
        flops=5_000_000_000,
    )


def assemble(parts):
    def body(refs, outs, _):
        for at in range(4):
            row, col = (3, 0)[at // 2], (6, 0)[at % 2]
            outs["out"][row : row + 3, col : col + 6] = refs[at][...]

    result = run(body, {"out": (6, 12, 4, 1024)}, dict(enumerate(parts)), limit=8)["out"]
    return result.transpose(2, 0, 1, 3)


def receive(array, lat, lon):
    rows, cols = lax.axis_size("lat"), lax.axis_size("lon")
    pairs = [
        (((a + lat) % rows) * cols + (b + lon) % cols, a * cols + b)
        for a in range(rows)
        for b in range(cols)
    ]
    return lax.ppermute(array, ("lat", "lon"), pairs)


AHEAD = {"lon": (0, 1), "lat": (1, 0), "both": (1, 1)}


def shift(pieces):
    return {name: receive(piece, *AHEAD[name]) for name, piece in pieces.items()}


def shards(fine, fine_qkv, fine_out, fine_up, fine_down, merge_weight, coarse_qkv, coarse_out):
    weights = {"qkv": fine_qkv, "out": fine_out, "up": fine_up, "down": fine_down}
    x = fine.reshape(4, 288, 512)
    sources = {"own": x} | shift(split_first(x))
    blocks = fine_quads(QUADS[:1], sources, weights, {}, ("both",))
    corners = shift({"both": blocks.pop("both")})["both"]
    sources["both"] = corners
    second = fine_quads(QUADS[1:3], sources, weights, blocks, ("lon", "lat"))
    pieces = shift({name: second.pop(name) for name in ("lon", "lat")}) | {"both": corners}
    blocks |= second
    blocks |= fine_quads(QUADS[3:], sources, weights, {}, ())
    parts = coarse(blocks, pieces, merge_weight, coarse_qkv, coarse_out)
    moved = [parts[0], receive(parts[1], 0, -1), receive(parts[2], -1, 0), receive(parts[3], -1, -1)]
    return assemble(moved)


def solution(mesh):
    in_specs = (P(None, "lat", "lon", None), P(), P(), P(), P(), P(), P(), P())
    out_specs = P(None, "lat", "lon", None)
    return jax.shard_map(shards, mesh=mesh, in_specs=in_specs, out_specs=out_specs, check_vma=False)
```

```python
import functools
import math

import jax
import jax.numpy as jnp
import numpy as np
from jax import lax
from jax.experimental import pallas as pl
from jax.experimental.pallas import tpu as pltpu
from jax.sharding import PartitionSpec as P

F32 = jnp.float32
BF16 = jnp.bfloat16
HEAD = 32
GROUP = 256
ORDER = (1, 2, 3, 0)
QUADS = ((0, 0), (0, 1), (1, 0), (1, 1))
EXP_SCALE = HEAD ** -0.5 * math.log2(math.e)
MIB = 1024 * 1024


def piece_of(i, j):
    if i >= 3 and j < 6:
        return "lon", (i - 3) * 6 + j
    if i < 3 and j >= 6:
        return "lat", i * 18 + j - 6
    if i < 3 and j < 6:
        return "both", i * 6 + j
    return None, 0


def source_of(i, j):
    i, j = i + 3, j + 6
    if i < 12 and j < 24:
        return "own", (i, j)
    return piece_of(i - 12 if i >= 12 else i, j - 24 if j >= 24 else j)


PIECE_ROWS = {"lon": 56, "lat": 56, "both": 24}


def first_send_table():
    row = lax.broadcasted_iota(jnp.int32, (112, 1), 0).astype(F32)

    def at(start, width, first_row, first_col):
        place = row - start
        line = jnp.floor((place + 0.5) / width)
        return (line + first_row) * 24 + (place - line * width) + first_col

    source = jnp.where(row < 56, at(0, 6, 3, 0), at(56, 18, 0, 6))
    lane = lax.broadcasted_iota(jnp.int32, (112, 288), 1).astype(F32)
    return (lane == source).astype(F32).astype(BF16)


OWN_ROWS = ((64, 224), (208, 288))
GATHER = (
    {"own": 0, "lon": 160},
    {"own": 0, "lon": 80, "lat": 144, "both": 208},
)


def window_table(quad):
    table, used = np.zeros((2, 80, 128), np.float32), set()
    for r in range(6):
        for c in range(12):
            name, at = source_of(quad[0] * 6 + r, quad[1] * 12 + c)
            used.add(name)
            if name == "own":
                at = at[0] * 24 + at[1] - OWN_ROWS[quad[0]][0]
            at += GATHER[quad[0]][name]
            table[at // 128, r * 12 + c, at % 128] = 1
    return table, sorted(used)


def second_send_tables(quad):
    tables = {}
    for r in range(6):
        for c in range(12):
            name, at = piece_of(quad[0] * 6 + r, quad[1] * 12 + c)
            if name is not None:
                tables.setdefault(name, np.zeros((80, 128), np.float32))[at, r * 12 + c] = 1
    return tables


PAIR_GATHER = {quad: 80 * at for at, quad in enumerate(QUADS)}
PAIR_GATHER |= {"lon": 320, "lat": 384, "both": 448}


def pair_tables():
    table = np.zeros((4, 288, 128), np.float32)
    for i in range(12):
        for j in range(24):
            to = ((i % 2) * 2 + j % 2) * 72 + (i // 2) * 12 + j // 2
            name, at = source_of(i, j)
            if name == "own":
                name, at = (at[0] // 6, at[1] // 12), (at[0] % 6) * 12 + at[1] % 12
            at += PAIR_GATHER[name]
            table[at // 128, to, at % 128] = 1
    return table


def last_send_table():
    table = np.zeros((3, 288, 96), np.float32)
    for place, level in enumerate(ORDER):
        for i in range(6):
            for j in range(12):
                part = (i // 3) * 2 + j // 6
                to, at = part * 72 + ((i % 3) * 6 + j % 6) * 4 + level, place * 72 + i * 12 + j
                table[at // 96, to, at % 96] = 1
    return table


def dot(a, b):
    return jnp.dot(a, b, preferred_element_type=F32)


def normalize(values):
    center = values - jnp.mean(values, -1, keepdims=True)
    spread = jnp.mean(center * center, -1, keepdims=True)
    return center * lax.rsqrt(spread + 1e-05)


def gelu(x):
    return 0.5 * x * (1.0 + lax.erf(x * 0.5**0.5))


def score(q, k):
    lane_head = lax.broadcasted_iota(jnp.int32, (1, GROUP), 1) // HEAD
    stacked = jnp.concatenate(
        [q * (lane_head == h).astype(BF16) for h in range(8)], axis=0
    )
    return lax.dot_general(k, stacked, (((1,), (1,)), ((), ())), preferred_element_type=F32)


def mix(scores, v, bias, first):
    if first is not None:
        scores = jnp.where(first, scores[:72], scores[72:])
    if bias is not None:
        scores = scores + bias[: scores.shape[0]]
    expo = jnp.exp2((scores - jnp.max(scores, 0, keepdims=True)) * EXP_SCALE)
    weights = expo * (1.0 / jnp.sum(expo, 0, keepdims=True))
    if first is not None:
        parts = [jnp.where(first, weights, 0.0), jnp.where(first, 0.0, weights)]
        weights = jnp.concatenate(parts, axis=0)
    full = lax.dot_general(
        weights.astype(BF16), v, (((0,), (0,)), ((), ())), preferred_element_type=F32
    )
    lane_head = lax.broadcasted_iota(jnp.int32, (1, GROUP), 1) // HEAD
    out = full[:144]
    for h in range(1, 8):
        out = jnp.where(lane_head == h, full[h * 144 : h * 144 + 144], out)
    return out.astype(BF16)


def attend(qkv, width, biases):
    lane = lax.broadcasted_iota(jnp.int32, (1, 1152), 1)
    first = lax.rem(lane, 144) < 72
    units = []
    for at, bias in enumerate(biases):
        for g in range(width // GROUP):
            for half in range(2):
                rows = slice(at * 288 + half * 144, at * 288 + half * 144 + 144)
                lanes = [
                    slice(part * width + g * GROUP, part * width + (g + 1) * GROUP)
                    for part in range(3)
                ]
                operands = [qkv[rows, s] for s in lanes]
                units.append((at, g, half, operands, bias, first if half else None))
    outs = {}
    ready = score(*units[0][3][:2])
    for at, (tile, g, half, operands, bias, alone) in enumerate(units):
        ahead = score(*units[at + 1][3][:2]) if at + 1 < len(units) else None
        outs[tile, half, g] = mix(ready, operands[2], bias, alone)
        ready = ahead
    rows = []
    for tile in range(len(biases)):
        for half in range(2):
            row = [outs[tile, half, g] for g in range(width // GROUP)]
            rows.append(jnp.concatenate(row, axis=1))
    return jnp.concatenate(rows, axis=0)


def fill_bias(bias):
    edge = lax.axis_index("lat") == lax.axis_size("lat") - 1
    large = jnp.where(edge, 5e29, 0.0).astype(F32)
    query = lax.rem(lax.broadcasted_iota(jnp.int32, (1, 1152), 1), 144)
    keys = lax.broadcasted_iota(jnp.int32, (144, 1), 0)
    sides = [
        jnp.where(jnp.where(place >= 72, place - 72, place) < 36, 1.0, -1.0)
        for place in (keys, query)
    ]
    bias[...] = (sides[0] * sides[1] - 1.0) * large


BIAS = pltpu.VMEM((144, 1152), F32)


def run(body, outs, ins, scratch=(), flops=0, limit=32):
    names, out_names = list(ins), list(outs)

    def kernel(*refs):
        first, last = len(names), len(names) + len(out_names)
        body(dict(zip(names, refs)), dict(zip(out_names, refs[first:last])), refs[last:])

    size = sum(math.prod(array.shape) * 2 for array in ins.values())
    results = pl.pallas_call(
        kernel,
        out_shape=[jax.ShapeDtypeStruct(shape, BF16) for shape in outs.values()],
        in_specs=[pl.BlockSpec(memory_space=pltpu.VMEM)] * len(names),
        out_specs=[pl.BlockSpec(memory_space=pltpu.VMEM)] * len(out_names),
        scratch_shapes=list(scratch),
        compiler_params=pltpu.CompilerParams(vmem_limit_bytes=limit * MIB),
        cost_estimate=pl.CostEstimate(flops=flops, bytes_accessed=size, transcendentals=0),
    )(*ins.values())
    return dict(zip(out_names, results))


def const(table):
    return jnp.asarray(table, BF16)


def split_first(x):
    def body(refs, outs, _):
        table = first_send_table()
        for level in range(4):
            rows = dot(table, refs["x"][level])
            outs["lon"][level] = rows[:56].astype(BF16)
            outs["lat"][level] = rows[56:].astype(BF16)

    return run(
        body,
        {name: (4, PIECE_ROWS[name], 512) for name in ("lon", "lat")},
        {"x": x},
        flops=10_000_000_000,
        limit=8,
    )


def corner_table():
    table = np.zeros((80, 128), np.float32)
    for i in range(3):
        for j in range(6):
            table[i * 6 + j, i * 24 + j] = 1
    return table


CHUNK = 1024


def fine_quads(quads, sources, weights, blocks, emit):
    tables = {quad: window_table(quad) for quad in quads}
    needed = sorted({name for quad in quads for name in tables[quad][1]})
    ins = {name: sources[name] for name in needed} | weights
    stack, place = [], {}
    for quad in quads:
        place[quad] = len(stack)
        stack += list(tables[quad][0])
    masked = any(quad[0] == 1 for quad in quads)
    outs = {quad: (4, 72, 512) for quad in quads}
    sends = {}
    if emit:
        for quad in QUADS:
            sends[quad] = second_send_tables(quad)
            sends[quad] = {name: sends[quad][name] for name in emit if name in sends[quad]}
            for name, table in sends[quad].items():
                place["send", quad, name] = len(stack)
                stack.append(table)
            if quad in blocks and sends[quad]:
                ins["block", quad] = blocks[quad]
        outs |= {name: (8 if name == "both" else 4, PIECE_ROWS[name], 512) for name in emit}
    if "both" in emit:
        place["corner"] = len(stack)
        stack.append(corner_table())
    ins["table"] = const(np.stack(stack))

    def body(refs, outs, scratch):
        gathered = scratch[0]
        gathered[...] = jnp.zeros_like(gathered)
        if masked:
            fill_bias(scratch[1])
        levels = []
        for at, quad in enumerate(quads):
            table = [refs["table"][place[quad] + part, :72, :] for part in range(2)]
            table = jnp.concatenate(table, axis=1)
            for level in ORDER:
                for name in tables[quad][1]:
                    rows = slice(*OWN_ROWS[quad[0]]) if name == "own" else slice(None)
                    source = refs[name][level, rows, :]
                    start = GATHER[quad[0]][name]
                    gathered[at * 4 + level, start : start + source.shape[0], :] = source
                levels.append(dot(table, gathered[at * 4 + level]))
        tokens = jnp.concatenate(levels, axis=0)
        qkv = dot(normalize(tokens).astype(BF16), refs["qkv"][...]).astype(BF16)
        mixed = attend(qkv, 512, [scratch[1] if quad[0] == 1 else None for quad in quads])
        hidden = (tokens + dot(mixed, refs["out"][...])).astype(BF16).astype(F32)
        normed = normalize(hidden).astype(BF16)
        total = hidden
        for at in range(0, 2048, CHUNK):
            inner = gelu(dot(normed, refs["up"][:, at : at + CHUNK])).astype(BF16)
            total = total + dot(inner, refs["down"][at : at + CHUNK, :])
        for at, quad in enumerate(quads):
            for place_at, level in enumerate(ORDER):
                start = at * 288 + place_at * 72
                outs[quad][level] = total[start : start + 72].astype(BF16)
        for name in emit:
            rows = PIECE_ROWS[name]
            for level in range(4):
                total = None
                for quad in QUADS:
                    if name in sends[quad]:
                        block = outs[quad] if quad in outs else refs["block", quad]
                        table = refs["table"][place["send", quad, name], :rows, :72]
                        term = dot(table, block[level])
                        total = term if total is None else total + term
                if name == "both":
                    corner = dot(refs["table"][place["corner"], :24, :80], refs["own"][level, :80, :])
                    outs[name][level] = corner.astype(BF16)
                outs[name][level + (4 if name == "both" else 0)] = total.astype(BF16)

    return run(
        body,
        outs,
        ins,
        [pltpu.VMEM((4 * len(quads), 256, 512), BF16)] + ([BIAS] if masked else []),
        flops=len(quads) * 2_500_000_000,
    )


def coarse(blocks, pieces, merge, qkv_weight, out_weight):
    sources = {("from", quad): blocks[quad] for quad in QUADS}
    sources |= {("from", name): pieces[name] for name in PIECE_ROWS}
    ins = sources | {"table": const(pair_tables()), "last": const(last_send_table())}
    ins |= {"merge": merge, "qkv": qkv_weight, "out": out_weight}

    def body(refs, outs, scratch):
        gathered, bias = scratch
        gathered[...] = jnp.zeros_like(gathered)
        fill_bias(bias)
        table = jnp.concatenate([refs["table"][at] for at in range(4)], axis=1)
        rows = []
        for level in ORDER:
            for name, start in PAIR_GATHER.items():
                source = refs["from", name][level + (4 if name == "both" else 0)]
                gathered[level, start : start + source.shape[0], :] = source
            total = dot(table, gathered[level])
            pairs = jnp.concatenate([total[72 * at : 72 * at + 72] for at in range(4)], axis=1)
            rows.append(normalize(pairs))
        pairs = jnp.concatenate(rows, axis=0).astype(BF16)
        merged = dot(pairs, refs["merge"][...]).astype(BF16).astype(F32)
        qkv = dot(normalize(merged).astype(BF16), refs["qkv"][...]).astype(BF16)
        mixed = attend(qkv, 1024, [bias])
        result = (merged + dot(mixed, refs["out"][...])).astype(BF16)
        parts = sum(dot(refs["last"][at], result[96 * at : 96 * at + 96]) for at in range(3))
        for part in range(4):
            for at in range(18):
                start = part * 72 + at * 4
                outs[part][at // 6, at % 6] = parts[start : start + 4].astype(BF16)

    return run(
        body,
        {part: (3, 6, 4, 1024) for part in range(4)},
        ins,
        [pltpu.VMEM((4, 512, 512), BF16), BIAS],
        flops=5_000_000_000,
    )


def assemble(parts):
    def body(refs, outs, _):
        for at in range(4):
            row, col = (3, 0)[at // 2], (6, 0)[at % 2]
            outs["out"][row : row + 3, col : col + 6] = refs[at][...]

    result = run(body, {"out": (6, 12, 4, 1024)}, dict(enumerate(parts)), limit=8)["out"]
    return result.transpose(2, 0, 1, 3)


def receive(array, lat, lon):
    rows, cols = lax.axis_size("lat"), lax.axis_size("lon")
    pairs = [
        (((a + lat) % rows) * cols + (b + lon) % cols, a * cols + b)
        for a in range(rows)
        for b in range(cols)
    ]
    return lax.ppermute(array, ("lat", "lon"), pairs)


AHEAD = {"lon": (0, 1), "lat": (1, 0), "both": (1, 1)}


def shift(pieces):
    return {name: receive(piece, *AHEAD[name]) for name, piece in pieces.items()}


def shards(fine, fine_qkv, fine_out, fine_up, fine_down, merge_weight, coarse_qkv, coarse_out):
    weights = {"qkv": fine_qkv, "out": fine_out, "up": fine_up, "down": fine_down}
    x = fine.reshape(4, 288, 512)
    sources = {"own": x} | shift(split_first(x))
    blocks = fine_quads(QUADS[:1], sources, weights, {}, ("both",))
    corners = shift({"both": blocks.pop("both")})["both"]
    sources["both"] = corners
    second = fine_quads(QUADS[1:2], sources, weights, blocks, ("lat",))
    pieces = {"both": corners} | shift({"lat": second.pop("lat")})
    third = fine_quads(QUADS[2:3], sources, weights, blocks, ("lon",))
    pieces |= shift({"lon": third.pop("lon")})
    blocks |= second | third
    blocks |= fine_quads(QUADS[3:], sources, weights, {}, ())
    parts = coarse(blocks, pieces, merge_weight, coarse_qkv, coarse_out)
    corner, lat = receive(parts[3], -1, -1), receive(parts[2], -1, 0)
    moved = [parts[0], receive(parts[1], 0, -1), lat, corner]
    return assemble(moved)


def solution(mesh):
    in_specs = (P(None, "lat", "lon", None), P(), P(), P(), P(), P(), P(), P())
    out_specs = P(None, "lat", "lon", None)
    return jax.shard_map(shards, mesh=mesh, in_specs=in_specs, out_specs=out_specs, check_vma=False)
```

```python
import functools
import math

import jax
import jax.numpy as jnp
import numpy as np
from jax import lax
from jax.experimental import pallas as pl
from jax.experimental.pallas import tpu as pltpu
from jax.sharding import PartitionSpec as P

F32 = jnp.float32
BF16 = jnp.bfloat16
HEAD = 32
GROUP = 256
ORDER = (1, 2, 3, 0)
QUADS = ((0, 0), (0, 1), (1, 0), (1, 1))
EXP_SCALE = HEAD ** -0.5 * math.log2(math.e)
MIB = 1024 * 1024


def piece_of(i, j):
    if i >= 3 and j < 6:
        return "lon", (i - 3) * 6 + j
    if i < 3 and j >= 6:
        return "lat", i * 18 + j - 6
    if i < 3 and j < 6:
        return "both", i * 6 + j
    return None, 0


def source_of(i, j):
    i, j = i + 3, j + 6
    if i < 12 and j < 24:
        return "own", (i, j)
    return piece_of(i - 12 if i >= 12 else i, j - 24 if j >= 24 else j)


PIECE_ROWS = {"lon": 56, "lat": 56, "both": 24}


def first_send_table():
    row = lax.broadcasted_iota(jnp.int32, (112, 1), 0).astype(F32)

    def at(start, width, first_row, first_col):
        place = row - start
        line = jnp.floor((place + 0.5) / width)
        return (line + first_row) * 24 + (place - line * width) + first_col

    source = jnp.where(row < 56, at(0, 6, 3, 0), at(56, 18, 0, 6))
    lane = lax.broadcasted_iota(jnp.int32, (112, 288), 1).astype(F32)
    return (lane == source).astype(F32).astype(BF16)


OWN_ROWS = ((64, 224), (208, 288))
GATHER = (
    {"own": 0, "lon": 160},
    {"own": 0, "lon": 80, "lat": 144, "both": 208},
)


def window_table(quad):
    table, used = np.zeros((2, 80, 128), np.float32), set()
    for r in range(6):
        for c in range(12):
            name, at = source_of(quad[0] * 6 + r, quad[1] * 12 + c)
            used.add(name)
            if name == "own":
                at = at[0] * 24 + at[1] - OWN_ROWS[quad[0]][0]
            at += GATHER[quad[0]][name]
            table[at // 128, r * 12 + c, at % 128] = 1
    return table, sorted(used)


def second_send_tables(quad):
    tables = {}
    for r in range(6):
        for c in range(12):
            name, at = piece_of(quad[0] * 6 + r, quad[1] * 12 + c)
            if name is not None:
                tables.setdefault(name, np.zeros((80, 128), np.float32))[at, r * 12 + c] = 1
    return tables


PAIR_GATHER = {quad: 80 * at for at, quad in enumerate(QUADS)}
PAIR_GATHER |= {"lon": 320, "lat": 384, "both": 448}


def pair_tables():
    table = np.zeros((4, 288, 128), np.float32)
    for i in range(12):
        for j in range(24):
            to = ((i % 2) * 2 + j % 2) * 72 + (i // 2) * 12 + j // 2
            name, at = source_of(i, j)
            if name == "own":
                name, at = (at[0] // 6, at[1] // 12), (at[0] % 6) * 12 + at[1] % 12
            at += PAIR_GATHER[name]
            table[at // 128, to, at % 128] = 1
    return table


def last_send_table():
    table = np.zeros((3, 288, 128), np.float32)
    for place, level in enumerate(ORDER):
        for i in range(6):
            for j in range(12):
                part = (i // 3) * 2 + j // 6
                to, at = part * 72 + ((i % 3) * 6 + j % 6) * 4 + level, place * 72 + i * 12 + j
                table[at // 128, to, at % 128] = 1
    return table


def dot(a, b):
    return jnp.dot(a, b, preferred_element_type=F32)


def normalize(values):
    center = values - jnp.mean(values, -1, keepdims=True)
    spread = jnp.mean(center * center, -1, keepdims=True)
    return center * lax.rsqrt(spread + 1e-05)


def gelu(x):
    return 0.5 * x * (1.0 + lax.erf(x * 0.5**0.5))


def score(q, k):
    lane_head = lax.broadcasted_iota(jnp.int32, (1, GROUP), 1) // HEAD
    stacked = jnp.concatenate(
        [q * (lane_head == h).astype(BF16) for h in range(8)], axis=0
    )
    return lax.dot_general(k, stacked, (((1,), (1,)), ((), ())), preferred_element_type=F32)


def mix(scores, v, bias, first):
    if first is not None:
        scores = jnp.where(first, scores[:72], scores[72:])
    if bias is not None:
        scores = scores + bias[: scores.shape[0]]
    expo = jnp.exp2((scores - jnp.max(scores, 0, keepdims=True)) * EXP_SCALE)
    weights = expo * (1.0 / jnp.sum(expo, 0, keepdims=True))
    if first is not None:
        parts = [jnp.where(first, weights, 0.0), jnp.where(first, 0.0, weights)]
        weights = jnp.concatenate(parts, axis=0)
    full = lax.dot_general(
        weights.astype(BF16), v, (((0,), (0,)), ((), ())), preferred_element_type=F32
    )
    lane_head = lax.broadcasted_iota(jnp.int32, (1, 128), 1) // HEAD
    halves = []
    for side in range(2):
        lanes = slice(side * 128, side * 128 + 128)
        out = full[side * 576 : side * 576 + 144, lanes]
        for h in range(1, 4):
            start = (side * 4 + h) * 144
            out = jnp.where(lane_head == h, full[start : start + 144, lanes], out)
        halves.append(out)
    return jnp.concatenate(halves, axis=1).astype(BF16)


def attend(qkv, width, biases):
    lane = lax.broadcasted_iota(jnp.int32, (1, 1152), 1)
    first = lax.rem(lane, 144) < 72
    units = []
    for at, bias in enumerate(biases):
        for g in range(width // GROUP):
            for half in range(2):
                rows = slice(at * 288 + half * 144, at * 288 + half * 144 + 144)
                lanes = [
                    slice(part * width + g * GROUP, part * width + (g + 1) * GROUP)
                    for part in range(3)
                ]
                operands = [qkv[rows, s] for s in lanes]
                units.append((at, g, half, operands, bias, first if half else None))
    outs = {}
    ready = score(*units[0][3][:2])
    for at, (tile, g, half, operands, bias, alone) in enumerate(units):
        ahead = score(*units[at + 1][3][:2]) if at + 1 < len(units) else None
        outs[tile, half, g] = mix(ready, operands[2], bias, alone)
        ready = ahead
    rows = []
    for tile in range(len(biases)):
        for half in range(2):
            row = [outs[tile, half, g] for g in range(width // GROUP)]
            rows.append(jnp.concatenate(row, axis=1))
    return jnp.concatenate(rows, axis=0)


def fill_bias(bias):
    edge = lax.axis_index("lat") == lax.axis_size("lat") - 1
    large = jnp.where(edge, 5e29, 0.0).astype(F32)
    query = lax.rem(lax.broadcasted_iota(jnp.int32, (1, 1152), 1), 144)
    keys = lax.broadcasted_iota(jnp.int32, (144, 1), 0)
    sides = [
        jnp.where(jnp.where(place >= 72, place - 72, place) < 36, 1.0, -1.0)
        for place in (keys, query)
    ]
    bias[...] = (sides[0] * sides[1] - 1.0) * large


BIAS = pltpu.VMEM((144, 1152), F32)


def run(body, outs, ins, scratch=(), flops=0, limit=32):
    names, out_names = list(ins), list(outs)

    def kernel(*refs):
        first, last = len(names), len(names) + len(out_names)
        body(dict(zip(names, refs)), dict(zip(out_names, refs[first:last])), refs[last:])

    size = sum(math.prod(array.shape) * 2 for array in ins.values())
    results = pl.pallas_call(
        kernel,
        out_shape=[jax.ShapeDtypeStruct(shape, BF16) for shape in outs.values()],
        in_specs=[pl.BlockSpec(memory_space=pltpu.VMEM)] * len(names),
        out_specs=[pl.BlockSpec(memory_space=pltpu.VMEM)] * len(out_names),
        scratch_shapes=list(scratch),
        compiler_params=pltpu.CompilerParams(vmem_limit_bytes=limit * MIB),
        cost_estimate=pl.CostEstimate(flops=flops, bytes_accessed=size, transcendentals=0),
    )(*ins.values())
    return dict(zip(out_names, results))


def const(table):
    return jnp.asarray(table, BF16)


def split_first(x):
    def body(refs, outs, _):
        table = first_send_table()
        for level in range(4):
            rows = dot(table, refs["x"][level])
            outs["lon"][level] = rows[:56].astype(BF16)
            outs["lat"][level] = rows[56:].astype(BF16)

    return run(
        body,
        {name: (4, PIECE_ROWS[name], 512) for name in ("lon", "lat")},
        {"x": x},
        flops=10_000_000_000,
        limit=8,
    )


def corner_table():
    table = np.zeros((80, 128), np.float32)
    for i in range(3):
        for j in range(6):
            table[i * 6 + j, i * 24 + j] = 1
    return table


CHUNK = 1024


def fine_quads(quads, sources, weights, blocks, emit):
    tables = {quad: window_table(quad) for quad in quads}
    needed = sorted({name for quad in quads for name in tables[quad][1]})
    ins = {name: sources[name] for name in needed} | weights
    stack, place = [], {}
    for quad in quads:
        place[quad] = len(stack)
        stack += list(tables[quad][0])
    masked = any(quad[0] == 1 for quad in quads)
    outs = {quad: (4, 72, 512) for quad in quads}
    sends = {}
    if emit:
        for quad in QUADS:
            sends[quad] = second_send_tables(quad)
            sends[quad] = {name: sends[quad][name] for name in emit if name in sends[quad]}
            for name, table in sends[quad].items():
                place["send", quad, name] = len(stack)
                stack.append(table)
            if quad in blocks and sends[quad]:
                ins["block", quad] = blocks[quad]
        outs |= {name: (8 if name == "both" else 4, PIECE_ROWS[name], 512) for name in emit}
    if "both" in emit:
        place["corner"] = len(stack)
        stack.append(corner_table())
    ins["table"] = const(np.stack(stack))

    def body(refs, outs, scratch):
        gathered = scratch[0]
        gathered[...] = jnp.zeros_like(gathered)
        if masked:
            fill_bias(scratch[1])
        levels = []
        for at, quad in enumerate(quads):
            table = [refs["table"][place[quad] + part, :72, :] for part in range(2)]
            table = jnp.concatenate(table, axis=1)
            for level in ORDER:
                for name in tables[quad][1]:
                    rows = slice(*OWN_ROWS[quad[0]]) if name == "own" else slice(None)
                    source = refs[name][level, rows, :]
                    start = GATHER[quad[0]][name]
                    gathered[at * 4 + level, start : start + source.shape[0], :] = source
                levels.append(dot(table, gathered[at * 4 + level]))
        tokens = jnp.concatenate(levels, axis=0)
        qkv = dot(normalize(tokens).astype(BF16), refs["qkv"][...]).astype(BF16)
        mixed = attend(qkv, 512, [scratch[1] if quad[0] == 1 else None for quad in quads])
        hidden = (tokens + dot(mixed, refs["out"][...])).astype(BF16).astype(F32)
        normed = normalize(hidden).astype(BF16)
        total = hidden
        for at in range(0, 2048, CHUNK):
            inner = gelu(dot(normed, refs["up"][:, at : at + CHUNK])).astype(BF16)
            total = total + dot(inner, refs["down"][at : at + CHUNK, :])
        for at, quad in enumerate(quads):
            for place_at, level in enumerate(ORDER):
                start = at * 288 + place_at * 72
                outs[quad][level] = total[start : start + 72].astype(BF16)
        for name in emit:
            rows = PIECE_ROWS[name]
            for level in range(4):
                total = None
                for quad in QUADS:
                    if name in sends[quad]:
                        block = outs[quad] if quad in outs else refs["block", quad]
                        table = refs["table"][place["send", quad, name], :rows, :72]
                        term = dot(table, block[level])
                        total = term if total is None else total + term
                if name == "both":
                    corner = dot(refs["table"][place["corner"], :24, :80], refs["own"][level, :80, :])
                    outs[name][level] = corner.astype(BF16)
                outs[name][level + (4 if name == "both" else 0)] = total.astype(BF16)

    return run(
        body,
        outs,
        ins,
        [pltpu.VMEM((4 * len(quads), 256, 512), BF16)] + ([BIAS] if masked else []),
        flops=len(quads) * 2_500_000_000,
    )


def coarse(blocks, pieces, merge, qkv_weight, out_weight):
    sources = {("from", quad): blocks[quad] for quad in QUADS}
    sources |= {("from", name): pieces[name] for name in PIECE_ROWS}
    ins = sources | {"table": const(pair_tables()), "last": const(last_send_table())}
    ins |= {"merge": merge, "qkv": qkv_weight, "out": out_weight}

    def body(refs, outs, scratch):
        gathered, bias = scratch
        gathered[...] = jnp.zeros_like(gathered)
        fill_bias(bias)
        table = jnp.concatenate([refs["table"][at] for at in range(4)], axis=1)
        rows = []
        for level in ORDER:
            for name, start in PAIR_GATHER.items():
                source = refs["from", name][level + (4 if name == "both" else 0)]
                gathered[level, start : start + source.shape[0], :] = source
            total = dot(table, gathered[level])
            pairs = jnp.concatenate([total[72 * at : 72 * at + 72] for at in range(4)], axis=1)
            rows.append(normalize(pairs))
        pairs = jnp.concatenate(rows, axis=0).astype(BF16)
        merged = dot(pairs, refs["merge"][...]).astype(BF16).astype(F32)
        qkv = dot(normalize(merged).astype(BF16), refs["qkv"][...]).astype(BF16)
        mixed = attend(qkv, 1024, [bias])
        result = (merged + dot(mixed, refs["out"][...])).astype(BF16)
        last = jnp.concatenate([refs["last"][at] for at in range(3)], axis=1)
        parts = dot(last[:, :288], result)
        for part in range(4):
            for at in range(18):
                start = part * 72 + at * 4
                outs[part][at // 6, at % 6] = parts[start : start + 4].astype(BF16)

    return run(
        body,
        {part: (3, 6, 4, 1024) for part in range(4)},
        ins,
        [pltpu.VMEM((4, 512, 512), BF16), BIAS],
        flops=5_000_000_000,
    )


def assemble(parts):
    def body(refs, outs, _):
        for at in range(4):
            row, col = (3, 0)[at // 2], (6, 0)[at % 2]
            outs["out"][row : row + 3, col : col + 6] = refs[at][...]

    result = run(body, {"out": (6, 12, 4, 1024)}, dict(enumerate(parts)), limit=8)["out"]
    return result.transpose(2, 0, 1, 3)


def receive(array, lat, lon):
    rows, cols = lax.axis_size("lat"), lax.axis_size("lon")
    pairs = [
        (((a + lat) % rows) * cols + (b + lon) % cols, a * cols + b)
        for a in range(rows)
        for b in range(cols)
    ]
    return lax.ppermute(array, ("lat", "lon"), pairs)


AHEAD = {"lon": (0, 1), "lat": (1, 0), "both": (1, 1)}


def shift(pieces):
    return {name: receive(piece, *AHEAD[name]) for name, piece in pieces.items()}


def shards(fine, fine_qkv, fine_out, fine_up, fine_down, merge_weight, coarse_qkv, coarse_out):
    weights = {"qkv": fine_qkv, "out": fine_out, "up": fine_up, "down": fine_down}
    x = fine.reshape(4, 288, 512)
    sources = {"own": x} | shift(split_first(x))
    blocks = fine_quads(QUADS[:1], sources, weights, {}, ("both",))
    corners = shift({"both": blocks.pop("both")})["both"]
    sources["both"] = corners
    second = fine_quads(QUADS[1:2], sources, weights, blocks, ("lat",))
    pieces = {"both": corners} | shift({"lat": second.pop("lat")})
    third = fine_quads(QUADS[2:3], sources, weights, blocks, ("lon",))
    pieces |= shift({"lon": third.pop("lon")})
    blocks |= second | third
    blocks |= fine_quads(QUADS[3:], sources, weights, {}, ())
    parts = coarse(blocks, pieces, merge_weight, coarse_qkv, coarse_out)
    corner, lat = receive(parts[3], -1, -1), receive(parts[2], -1, 0)
    moved = [parts[0], receive(parts[1], 0, -1), lat, corner]
    return assemble(moved)


def solution(mesh):
    in_specs = (P(None, "lat", "lon", None), P(), P(), P(), P(), P(), P(), P())
    out_specs = P(None, "lat", "lon", None)
    return jax.shard_map(shards, mesh=mesh, in_specs=in_specs, out_specs=out_specs, check_vma=False)
```

```python
import functools
import math

import jax
import jax.numpy as jnp
import numpy as np
from jax import lax
from jax.experimental import pallas as pl
from jax.experimental.pallas import tpu as pltpu
from jax.sharding import PartitionSpec as P

F32 = jnp.float32
BF16 = jnp.bfloat16
HEAD = 32
GROUP = 256
ORDER = (1, 2, 3, 0)
QUADS = ((0, 0), (0, 1), (1, 0), (1, 1))
EXP_SCALE = HEAD ** -0.5 * math.log2(math.e)
MIB = 1024 * 1024


def piece_of(i, j):
    if i >= 3 and j < 6:
        return "lon", (i - 3) * 6 + j
    if i < 3 and j >= 6:
        return "lat", i * 18 + j - 6
    if i < 3 and j < 6:
        return "both", i * 6 + j
    return None, 0


def source_of(i, j):
    i, j = i + 3, j + 6
    if i < 12 and j < 24:
        return "own", (i, j)
    return piece_of(i - 12 if i >= 12 else i, j - 24 if j >= 24 else j)


PIECE_ROWS = {"lon": 56, "lat": 56, "both": 24}


def first_send_table():
    row = lax.broadcasted_iota(jnp.int32, (112, 1), 0).astype(F32)

    def at(start, width, first_row, first_col):
        place = row - start
        line = jnp.floor((place + 0.5) / width)
        return (line + first_row) * 24 + (place - line * width) + first_col

    source = jnp.where(row < 56, at(0, 6, 3, 0), at(56, 18, 0, 6))
    lane = lax.broadcasted_iota(jnp.int32, (112, 288), 1).astype(F32)
    return (lane == source).astype(F32).astype(BF16)


OWN_ROWS = ((64, 224), (208, 288))
GATHER = (
    {"own": 0, "lon": 160},
    {"own": 0, "lon": 80, "lat": 144, "both": 208},
)


def window_table(quad):
    table, used = np.zeros((2, 80, 128), np.float32), set()
    for r in range(6):
        for c in range(12):
            name, at = source_of(quad[0] * 6 + r, quad[1] * 12 + c)
            used.add(name)
            if name == "own":
                at = at[0] * 24 + at[1] - OWN_ROWS[quad[0]][0]
            at += GATHER[quad[0]][name]
            table[at // 128, r * 12 + c, at % 128] = 1
    return table, sorted(used)


def second_send_tables(quad):
    tables = {}
    for r in range(6):
        for c in range(12):
            name, at = piece_of(quad[0] * 6 + r, quad[1] * 12 + c)
            if name is not None:
                tables.setdefault(name, np.zeros((80, 128), np.float32))[at, r * 12 + c] = 1
    return tables


PAIR_GATHER = {quad: 80 * at for at, quad in enumerate(QUADS)}
PAIR_GATHER |= {"lon": 320, "lat": 384, "both": 448}


def pair_tables():
    table = np.zeros((4, 288, 128), np.float32)
    for i in range(12):
        for j in range(24):
            to = ((i % 2) * 2 + j % 2) * 72 + (i // 2) * 12 + j // 2
            name, at = source_of(i, j)
            if name == "own":
                name, at = (at[0] // 6, at[1] // 12), (at[0] % 6) * 12 + at[1] % 12
            at += PAIR_GATHER[name]
            table[at // 128, to, at % 128] = 1
    return table


def last_send_table():
    table = np.zeros((3, 288, 128), np.float32)
    for place, level in enumerate(ORDER):
        for i in range(6):
            for j in range(12):
                part = (i // 3) * 2 + j // 6
                to, at = part * 72 + ((i % 3) * 6 + j % 6) * 4 + level, place * 72 + i * 12 + j
                table[at // 128, to, at % 128] = 1
    return table


def dot(a, b):
    return jnp.dot(a, b, preferred_element_type=F32)


def normalize(values):
    center = values - jnp.mean(values, -1, keepdims=True)
    spread = jnp.mean(center * center, -1, keepdims=True)
    return center * lax.rsqrt(spread + 1e-05)


def gelu(x):
    return 0.5 * x * (1.0 + lax.erf(x * 0.5**0.5))


def score(q, k):
    lane_head = lax.broadcasted_iota(jnp.int32, (1, GROUP), 1) // HEAD
    stacked = jnp.concatenate(
        [q * (lane_head == h).astype(BF16) for h in range(8)], axis=0
    )
    return lax.dot_general(k, stacked, (((1,), (1,)), ((), ())), preferred_element_type=F32)


def mix(scores, v, bias, first):
    if first is not None:
        scores = jnp.where(first, scores[:72], scores[72:])
    if bias is not None:
        scores = scores + bias[: scores.shape[0]]
    expo = jnp.exp2((scores - jnp.max(scores, 0, keepdims=True)) * EXP_SCALE)
    weights = expo * (1.0 / jnp.sum(expo, 0, keepdims=True))
    if first is not None:
        parts = [jnp.where(first, weights, 0.0), jnp.where(first, 0.0, weights)]
        weights = jnp.concatenate(parts, axis=0)
    full = lax.dot_general(
        weights.astype(BF16), v, (((0,), (0,)), ((), ())), preferred_element_type=F32
    )
    lane_head = lax.broadcasted_iota(jnp.int32, (1, 128), 1) // HEAD
    halves = []
    for side in range(2):
        lanes = slice(side * 128, side * 128 + 128)
        out = full[side * 576 : side * 576 + 144, lanes]
        for h in range(1, 4):
            start = (side * 4 + h) * 144
            out = jnp.where(lane_head == h, full[start : start + 144, lanes], out)
        halves.append(out)
    return jnp.concatenate(halves, axis=1).astype(BF16)


def attend(qkv, width, biases):
    lane = lax.broadcasted_iota(jnp.int32, (1, 1152), 1)
    first = lax.rem(lane, 144) < 72
    units = []
    for at, bias in enumerate(biases):
        for g in range(width // GROUP):
            for half in range(2):
                rows = slice(at * 288 + half * 144, at * 288 + half * 144 + 144)
                lanes = [
                    slice(part * width + g * GROUP, part * width + (g + 1) * GROUP)
                    for part in range(3)
                ]
                operands = [qkv[rows, s] for s in lanes]
                units.append((at, g, half, operands, bias, first if half else None))
    outs = {}
    ready = score(*units[0][3][:2])
    for at, (tile, g, half, operands, bias, alone) in enumerate(units):
        ahead = score(*units[at + 1][3][:2]) if at + 1 < len(units) else None
        outs[tile, half, g] = mix(ready, operands[2], bias, alone)
        ready = ahead
    rows = []
    for tile in range(len(biases)):
        for half in range(2):
            row = [outs[tile, half, g] for g in range(width // GROUP)]
            rows.append(jnp.concatenate(row, axis=1))
    return jnp.concatenate(rows, axis=0)


def fill_bias(bias):
    edge = lax.axis_index("lat") == lax.axis_size("lat") - 1
    large = jnp.where(edge, 5e29, 0.0).astype(F32)
    query = lax.rem(lax.broadcasted_iota(jnp.int32, (1, 1152), 1), 144)
    keys = lax.broadcasted_iota(jnp.int32, (144, 1), 0)
    sides = [
        jnp.where(jnp.where(place >= 72, place - 72, place) < 36, 1.0, -1.0)
        for place in (keys, query)
    ]
    bias[...] = (sides[0] * sides[1] - 1.0) * large


BIAS = pltpu.VMEM((144, 1152), F32)


def run(body, outs, ins, scratch=(), flops=0, limit=32):
    names, out_names = list(ins), list(outs)

    def kernel(*refs):
        first, last = len(names), len(names) + len(out_names)
        body(dict(zip(names, refs)), dict(zip(out_names, refs[first:last])), refs[last:])

    size = sum(math.prod(array.shape) * 2 for array in ins.values())
    results = pl.pallas_call(
        kernel,
        out_shape=[jax.ShapeDtypeStruct(shape, BF16) for shape in outs.values()],
        in_specs=[pl.BlockSpec(memory_space=pltpu.VMEM)] * len(names),
        out_specs=[pl.BlockSpec(memory_space=pltpu.VMEM)] * len(out_names),
        scratch_shapes=list(scratch),
        compiler_params=pltpu.CompilerParams(vmem_limit_bytes=limit * MIB),
        cost_estimate=pl.CostEstimate(flops=flops, bytes_accessed=size, transcendentals=0),
    )(*ins.values())
    return dict(zip(out_names, results))


def const(table):
    return jnp.asarray(table, BF16)


def split_first(x):
    def body(refs, outs, _):
        table = first_send_table()
        for level in range(4):
            rows = dot(table, refs["x"][level])
            outs["lon"][level] = rows[:56].astype(BF16)
            outs["lat"][level] = rows[56:].astype(BF16)

    return run(
        body,
        {name: (4, PIECE_ROWS[name], 512) for name in ("lon", "lat")},
        {"x": x},
        flops=10_000_000_000,
        limit=8,
    )


def corner_table():
    table = np.zeros((80, 128), np.float32)
    for i in range(3):
        for j in range(6):
            table[i * 6 + j, i * 24 + j] = 1
    return table


CHUNK = 1024


def fine_quads(quads, sources, weights, blocks, emit):
    tables = {quad: window_table(quad) for quad in quads}
    needed = sorted({name for quad in quads for name in tables[quad][1]})
    ins = {name: sources[name] for name in needed} | weights
    stack, place = [], {}
    for quad in quads:
        place[quad] = len(stack)
        stack += list(tables[quad][0])
    masked = any(quad[0] == 1 for quad in quads)
    outs = {quad: (4, 72, 512) for quad in quads}
    sends = {}
    if emit:
        for quad in QUADS:
            sends[quad] = second_send_tables(quad)
            sends[quad] = {name: sends[quad][name] for name in emit if name in sends[quad]}
            for name, table in sends[quad].items():
                place["send", quad, name] = len(stack)
                stack.append(table)
            if quad in blocks and sends[quad]:
                ins["block", quad] = blocks[quad]
        outs |= {name: (8 if name == "both" else 4, PIECE_ROWS[name], 512) for name in emit}
    if "both" in emit:
        place["corner"] = len(stack)
        stack.append(corner_table())
    ins["table"] = const(np.stack(stack))

    def body(refs, outs, scratch):
        gathered = scratch[0]
        gathered[...] = jnp.zeros_like(gathered)
        if masked:
            fill_bias(scratch[1])
        levels = []
        for at, quad in enumerate(quads):
            table = [refs["table"][place[quad] + part, :72, :] for part in range(2)]
            table = jnp.concatenate(table, axis=1)
            for level in ORDER:
                for name in tables[quad][1]:
                    rows = slice(*OWN_ROWS[quad[0]]) if name == "own" else slice(None)
                    source = refs[name][level, rows, :]
                    start = GATHER[quad[0]][name]
                    gathered[at * 4 + level, start : start + source.shape[0], :] = source
                levels.append(dot(table, gathered[at * 4 + level]))
        tokens = jnp.concatenate(levels, axis=0)
        qkv = dot(normalize(tokens).astype(BF16), refs["qkv"][...]).astype(BF16)
        mixed = attend(qkv, 512, [scratch[1] if quad[0] == 1 else None for quad in quads])
        hidden = (tokens + dot(mixed, refs["out"][...])).astype(BF16).astype(F32)
        normed = normalize(hidden).astype(BF16)
        total = hidden
        for at in range(0, 2048, CHUNK):
            inner = gelu(dot(normed, refs["up"][:, at : at + CHUNK])).astype(BF16)
            total = total + dot(inner, refs["down"][at : at + CHUNK, :])
        for at, quad in enumerate(quads):
            for place_at, level in enumerate(ORDER):
                start = at * 288 + place_at * 72
                outs[quad][level] = total[start : start + 72].astype(BF16)
        for name in emit:
            rows = PIECE_ROWS[name]
            for level in range(4):
                total = None
                for quad in QUADS:
                    if name in sends[quad]:
                        block = outs[quad] if quad in outs else refs["block", quad]
                        table = refs["table"][place["send", quad, name], :rows, :72]
                        term = dot(table, block[level])
                        total = term if total is None else total + term
                if name == "both":
                    corner = dot(refs["table"][place["corner"], :24, :80], refs["own"][level, :80, :])
                    outs[name][level] = corner.astype(BF16)
                outs[name][level + (4 if name == "both" else 0)] = total.astype(BF16)

    return run(
        body,
        outs,
        ins,
        [pltpu.VMEM((4 * len(quads), 256, 512), BF16)] + ([BIAS] if masked else []),
        flops=len(quads) * 2_500_000_000,
    )


def coarse(blocks, pieces, merge, qkv_weight, out_weight):
    sources = {("from", quad): blocks[quad] for quad in QUADS}
    sources |= {("from", name): pieces[name] for name in PIECE_ROWS}
    ins = sources | {"table": const(pair_tables()), "last": const(last_send_table())}
    ins |= {"merge": merge, "qkv": qkv_weight, "out": out_weight}

    def body(refs, outs, scratch):
        gathered, bias = scratch
        gathered[...] = jnp.zeros_like(gathered)
        fill_bias(bias)
        table = jnp.concatenate([refs["table"][at] for at in range(4)], axis=1)
        rows = []
        for level in ORDER:
            for name, start in PAIR_GATHER.items():
                source = refs["from", name][level + (4 if name == "both" else 0)]
                gathered[level, start : start + source.shape[0], :] = source
            total = dot(table, gathered[level])
            pairs = jnp.concatenate([total[72 * at : 72 * at + 72] for at in range(4)], axis=1)
            rows.append(normalize(pairs))
        pairs = jnp.concatenate(rows, axis=0).astype(BF16)
        merged = dot(pairs, refs["merge"][...]).astype(BF16).astype(F32)
        qkv = dot(normalize(merged).astype(BF16), refs["qkv"][...]).astype(BF16)
        mixed = attend(qkv, 1024, [bias])
        result = (merged + dot(mixed, refs["out"][...])).astype(BF16)
        last = jnp.concatenate([refs["last"][at] for at in range(3)], axis=1)
        parts = dot(last[:, :288], result)
        for part in range(4):
            for at in range(18):
                start = part * 72 + at * 4
                outs[part][at // 6, at % 6] = parts[start : start + 4].astype(BF16)

    return run(
        body,
        {part: (3, 6, 4, 1024) for part in range(4)},
        ins,
        [pltpu.VMEM((4, 512, 512), BF16), BIAS],
        flops=5_000_000_000,
    )


def assemble(parts):
    def body(refs, outs, _):
        for at in range(4):
            row, col = (3, 0)[at // 2], (6, 0)[at % 2]
            outs["out"][row : row + 3, col : col + 6] = refs[at][...]

    result = run(body, {"out": (6, 12, 4, 1024)}, dict(enumerate(parts)), limit=8)["out"]
    return result.transpose(2, 0, 1, 3)


def receive(array, lat, lon):
    rows, cols = lax.axis_size("lat"), lax.axis_size("lon")
    pairs = [
        (((a + lat) % rows) * cols + (b + lon) % cols, a * cols + b)
        for a in range(rows)
        for b in range(cols)
    ]
    return lax.ppermute(array, ("lat", "lon"), pairs)


AHEAD = {"lon": (0, 1), "lat": (1, 0), "both": (1, 1)}


def shift(pieces):
    return {name: receive(piece, *AHEAD[name]) for name, piece in pieces.items()}


def shards(fine, fine_qkv, fine_out, fine_up, fine_down, merge_weight, coarse_qkv, coarse_out):
    weights = {"qkv": fine_qkv, "out": fine_out, "up": fine_up, "down": fine_down}
    x = fine.reshape(4, 288, 512)
    sources = {"own": x} | shift(split_first(x))
    blocks = fine_quads(QUADS[:1], sources, weights, {}, ("both",))
    corners = shift({"both": blocks.pop("both")})["both"]
    sources["both"] = corners
    second = fine_quads(QUADS[2:3], sources, weights, blocks, ("lon",))
    pieces = {"both": corners} | shift({"lon": second.pop("lon")})
    third = fine_quads(QUADS[1:2], sources, weights, blocks, ("lat",))
    pieces |= shift({"lat": third.pop("lat")})
    blocks |= second | third
    blocks |= fine_quads(QUADS[3:], sources, weights, {}, ())
    parts = coarse(blocks, pieces, merge_weight, coarse_qkv, coarse_out)
    corner, lat = receive(parts[3], -1, -1), receive(parts[2], -1, 0)
    moved = [parts[0], receive(parts[1], 0, -1), lat, corner]
    return assemble(moved)


def solution(mesh):
    in_specs = (P(None, "lat", "lon", None), P(), P(), P(), P(), P(), P(), P())
    out_specs = P(None, "lat", "lon", None)
    return jax.shard_map(shards, mesh=mesh, in_specs=in_specs, out_specs=out_specs, check_vma=False)
```
